512 devices in a mesh: pts: 128 (over z, y, core), grp: 4 (over x).
Axes of the slice: x: 4, y: 4, z: 16, core: 2. Of those that a mesh axis runs over, the one named last changes fastest.
Arguments:
- feats4: bfloat16 [262144, 256], P(('pts', 'grp')), may hold values from -6 to 6
- order4: int32 [262144], P(('pts', 'grp')), may hold values from 0 to 262143, as said below
- gain4: float32 [256], replicated, may hold values from 0.25 to 1.75
- qkv4: bfloat16 [3, 256, 256], replicated
- proj4: bfloat16 [256, 256], replicated, may hold values from -0.375 to 0.375
- pool_weight: bfloat16 [256, 512], replicated, may hold values from -0.375 to 0.375
- child5: int32 [65536, 8], P('pts'), may hold values from 0 to 262143, as said below
- mask5: int32 [65536, 8], P('pts'), may hold values from 0 to 1, as said below
- order5: int32 [65536], P('pts'), may hold values from 0 to 65535, as said below
- gain5: float32 [512], replicated, may hold values from 0.25 to 1.75
- qkv5: bfloat16 [3, 512, 512], P(None, None, 'grp')
- proj5: bfloat16 [512, 512], P('grp'), may hold values from -0.25 to 0.25
Outputs:
- fine_out: bfloat16 [262144, 256], P(('pts', 'grp'))
- coarse_out: bfloat16 [65536, 512], P('pts', 'grp')
The draws below stay inside these ranges and needn't reach their ends.
Inputs may be any that keep to these rules, and one draw needn't show every extreme that they name: `order4`: A permutation of the 262144 section-4 rows; the 512 curve positions of one device take exactly 1 row from the owner rows of each device. Section-5 point i has c children, c from 1 to 8: the consecutive section-4 curve positions child5[i, 0] to child5[i, 0] + c - 1 in slots 0 to c - 1; later slots hold arbitrary section-4 curve positions of the same index of pts. The children of the 512 points of one index of pts are the 2048 section-4 curve positions of that index, each once, in the order of the points. Every index of pts has a point with 8 children. `mask5`: 1 exactly on the slots that hold children. `order5`: A permutation of the 65536 pooled rows; the 512 curve positions of one index of pts take exactly 4 rows from the pooled rows of each index.
All inputs are finite; a program needn't handle non-finite values.
Results may differ from the reference program's by a relative error of at most 0.022.
The reference program's roundings to bfloat16 on the way count: a program that leaves them out, or rounds other values in their place, can miss the bound.
Values may be sent and summed in bfloat16 or wider, within the bound.
No kernel may reach another device: no remote copies, remote signals or barrier semaphores. Data moves between devices by JAX's collectives and lax.ppermute only.
A program may use at most 64 MiB of HBM per device.

```python
import math
import jax
import jax.numpy as jnp
from jax import lax

C4 = 256
H4 = 16
C5 = 512
H5 = 32
PATCH = 1024
KIDS = 8
R4 = 512
R5 = 512
N4 = 262144
N5 = 65536
N_PTS = 128
N_GRP = 4


PATTERNS = ((8, 4, 3, 1), (4, 4, 4, 4), (6, 2, 5, 3), (7, 1, 2, 6), (5, 5, 3, 3), (8, 1, 1, 6), (2, 2, 6, 6), (3, 4, 7, 2))


def kid_counts(key):
    pick_key, shuffle_key = jax.random.split(jax.random.fold_in(key, 101))
    groups = R5 // 4
    drawn_patterns = jax.random.randint(pick_key, (N_PTS, groups), 0, len(PATTERNS))
    column = jnp.arange(groups)[None, :]
    picked = jnp.where(column == 0, 0, drawn_patterns)
    pattern_table = jnp.array(PATTERNS, jnp.int32)
    counts = pattern_table[picked].reshape(N_PTS, R5)
    shuffles = jax.vmap(lambda piece_key: jax.random.permutation(piece_key, R5))(jax.random.split(shuffle_key, N_PTS))
    return jnp.take_along_axis(counts, shuffles, axis=1)


def dealt_order(key, blocks, rows):
    per_peer = rows // blocks
    owner_key, place_key = jax.random.split(key)
    owner_perm = jax.vmap(lambda piece_key: jax.random.permutation(piece_key, rows))(jax.random.split(owner_key, blocks))
    spread = owner_perm.reshape(blocks, blocks, per_peer).transpose(1, 0, 2)
    owner_base = (jnp.arange(blocks) * rows)[None, :, None]
    table_rows = (spread + owner_base).reshape(blocks, rows)
    places = jax.vmap(lambda piece_key: jax.random.permutation(piece_key, rows))(jax.random.split(place_key, blocks))
    return jnp.take_along_axis(table_rows, places, axis=1).reshape(blocks * rows).astype(jnp.int32)


def attention_weight(key, width):
    query_key = jax.random.fold_in(key, 2)
    probe_key = jax.random.fold_in(key, 3)
    value_key = jax.random.fold_in(key, 4)
    query_part = jax.random.normal(query_key, (width, width), jnp.float32) / math.sqrt(width)
    probe_part = jax.random.normal(probe_key, (width, width), jnp.float32) / math.sqrt(width)
    value_part = jax.random.normal(value_key, (width, width), jnp.float32) / math.sqrt(width)
    return jnp.stack([query_part, probe_part, value_part]).astype(jnp.bfloat16)


def draw_order4(key, part):
    key = jax.random.fold_in(key, 7)
    return dealt_order(key, N_PTS * N_GRP, R4)


def draw_order5(key, part):
    key = jax.random.fold_in(key, 11)
    return dealt_order(key, N_PTS, R5)


def draw_child5(key, part):
    counts = kid_counts(key)
    key = jax.random.fold_in(key, 3)
    starts = jnp.cumsum(counts, axis=1) - counts
    block_base = (jnp.arange(N_PTS) * (N_GRP * R4))[:, None]
    first_kid = (block_base + starts)[:, :, None]
    slot_index = jnp.arange(KIDS)[None, None, :]
    filler = jax.random.randint(key, (N_PTS, R5, KIDS), 0, N_GRP * R4) + block_base[:, :, None]
    kid_index = jnp.where(slot_index < counts[:, :, None], first_kid + slot_index, filler)
    return kid_index.reshape(N5, KIDS).astype(jnp.int32)


def draw_mask5(key, part):
    counts = kid_counts(key)
    slot_index = jnp.arange(KIDS)[None, None, :]
    return (slot_index < counts[:, :, None]).astype(jnp.int32).reshape(N5, KIDS)


def draw_qkv4(key, part):
    key = jax.random.fold_in(key, 13)
    return attention_weight(key, C4)


def draw_qkv5(key, part):
    key = jax.random.fold_in(key, 17)
    return attention_weight(key, C5)


def block_scale(stream_key, dims, shards, low, high):
    factor_of = 1.0
    for dim, shards_of in shards:
        steps = jax.random.uniform(jax.random.fold_in(jax.random.fold_in(stream_key, 6), dim), (shards_of,), jnp.float32, low / len(shards), high / len(shards))
        factor_of = factor_of * jnp.repeat(jnp.exp(steps), dims[dim] // shards_of).reshape((-1,) + (1,) * (len(dims) - 1 - dim))
    return factor_of


def noise(stream_key, dims, scale, bound, cuts=(), held_as=jnp.bfloat16):
    values = scale * jax.random.normal(stream_key, dims, jnp.float32)
    if cuts:
        values = values * block_scale(stream_key, dims, cuts, -0.22, 0.18)
    return jnp.clip(values, -bound, bound).astype(held_as)


def setup_inputs(seed: int = 0) -> dict:
    key_of = jax.random.split(jax.random.key(seed), 13)
    return {
        "feats4": noise(key_of[0], (N4, C4), 1.0, 6.0, ((0, 512),)),
        "order4": draw_order4(jax.random.fold_in(key_of[12], 71), 0),
        "gain4": jnp.clip(1.0 + 0.15 * jax.random.normal(key_of[2], (C4,), jnp.float32), 0.25, 1.75),
        "qkv4": draw_qkv4(jax.random.fold_in(key_of[12], 71), 0),
        "proj4": noise(key_of[4], (C4, C4), C4 ** -0.5, 0.375),
        "pool_weight": noise(key_of[5], (C4, C5), C4 ** -0.5, 0.375),
        "child5": draw_child5(jax.random.fold_in(key_of[12], 71), 0),
        "mask5": draw_mask5(jax.random.fold_in(key_of[12], 71), 0),
        "order5": draw_order5(jax.random.fold_in(key_of[12], 71), 0),
        "gain5": jnp.clip(1.0 + 0.15 * jax.random.normal(key_of[9], (C5,), jnp.float32), 0.25, 1.75),
        "qkv5": draw_qkv5(jax.random.fold_in(key_of[12], 71), 0),
        "proj5": noise(key_of[11], (C5, C5), C5 ** -0.5, 0.25, ((0, 4),)),
    }


epsilon = 1e-05

def layer_norm(rows_in, norm_gain):
    values = rows_in.astype(jnp.float32)
    center = values - lax.optimization_barrier(jnp.mean(values, axis=-1, keepdims=True))
    spread = lax.optimization_barrier(jnp.mean(center * center, axis=-1, keepdims=True))
    return (center * lax.rsqrt(spread + epsilon) * norm_gain).astype(jnp.bfloat16)

def patch_heads(queries, key_rows, value_rows, head_count):
    row_count = queries.shape[0]
    head_size = queries.shape[1] // head_count
    split_query = queries.astype(jnp.float32).reshape(row_count, head_count, head_size)
    split_key = key_rows.astype(jnp.float32).reshape(row_count, head_count, head_size)
    split_value = value_rows.astype(jnp.float32).reshape(row_count, head_count, head_size)
    scores = jnp.einsum('qhd,khd->hqk', split_query, split_key) * (1.0 / math.sqrt(head_size))
    row_max = lax.optimization_barrier(jnp.max(scores, axis=-1, keepdims=True))
    weights = jnp.exp(scores - row_max)
    probabilities = (weights / lax.optimization_barrier(jnp.sum(weights, axis=-1, keepdims=True))).astype(jnp.bfloat16)
    mixed_heads = jnp.einsum('hqk,khd->qhd', probabilities.astype(jnp.float32), split_value)
    return mixed_heads.astype(jnp.bfloat16).reshape(row_count, head_count * head_size)

def attention_all(projected, head_count):
    total_rows = projected.shape[1]
    width = projected.shape[2]
    patches = projected.reshape(3, total_rows // PATCH, PATCH, width).transpose(1, 0, 2, 3)

    def one_patch(triple):
        return patch_heads(triple[0], triple[1], triple[2], head_count)
    return lax.map(one_patch, patches).reshape(total_rows, width)

def project_three(normed, weights):
    parts = [jnp.dot(normed, weights[index], preferred_element_type=jnp.float32).astype(jnp.bfloat16) for index in range(3)]
    return jnp.stack(parts)

def reference(feats4, order4, gain4, qkv4, proj4, pool_weight, child5, mask5, order5, gain5, qkv5, proj5):
    curve_rows = feats4[order4]
    normed4 = layer_norm(curve_rows, gain4)
    projected4 = project_three(normed4, qkv4)
    attended4 = attention_all(projected4, H4)
    fine_out = (curve_rows.astype(jnp.float32) + jnp.dot(attended4, proj4, preferred_element_type=jnp.float32)).astype(jnp.bfloat16)

    def pool_block(block_rows):
        kid_index, kid_flags = block_rows
        lifted = jnp.dot(fine_out[kid_index], pool_weight, preferred_element_type=jnp.float32)
        return lax.optimization_barrier(jnp.max(jnp.where(kid_flags[..., None] > 0, lifted, -jnp.inf), axis=1))
    pooled_max = lax.map(pool_block, (child5.reshape(N_PTS, -1, KIDS), mask5.reshape(N_PTS, -1, KIDS))).reshape(N5, C5)
    pooled = jax.nn.gelu(pooled_max, approximate=True).astype(jnp.bfloat16)
    coarse_rows = pooled[order5]
    normed5 = layer_norm(coarse_rows, gain5)
    projected5 = project_three(normed5, qkv5)
    attended5 = attention_all(projected5, H5)
    coarse_out = (coarse_rows.astype(jnp.float32) + jnp.dot(attended5, proj5, preferred_element_type=jnp.float32)).astype(jnp.bfloat16)
    return (fine_out, coarse_out)
```

```python
import functools
import math

import jax
import jax.numpy as jnp
from jax import lax
from jax.experimental import pallas as pl
from jax.experimental.pallas import tpu as pltpu
from jax.sharding import Mesh
from jax.sharding import PartitionSpec as P

C4 = 256
H4 = 16
C5 = 512
H5 = 32
HEAD = 16
KIDS = 8

epsilon = 1e-05
f32 = jnp.float32
bf16 = jnp.bfloat16

PTS = ("z", "y", "c")
PLANE = ("y", "c", "x")
ALL = ("z", "y", "c", "x")


def dot(a, b):
    return jnp.dot(a, b, preferred_element_type=f32)


def column(row):
    return jnp.transpose(jnp.broadcast_to(row, (8, row.shape[1])))[:, :1]


def one_hot(col, width):
    lanes = lax.broadcasted_iota(jnp.int32, (col.shape[0], width), 1)
    return jnp.where(col == lanes, 1.0, 0.0).astype(bf16)


def layer_norm(rows_in, norm_gain):
    values = rows_in.astype(f32)
    center = values - jnp.mean(values, axis=-1, keepdims=True)
    spread = jnp.mean(center * center, axis=-1, keepdims=True)
    return (center * lax.rsqrt(spread + epsilon) * norm_gain).astype(bf16)


def params(mib=48):
    return pltpu.CompilerParams(vmem_limit_bytes=mib << 20)


def request_kernel(order4_ref, order5_ref, out_ref, slot_ref):
    n = order4_ref.shape[1]
    x = lax.axis_index("x")
    owner4 = column(order4_ref[...] // n)
    rem4 = column(order4_ref[...] % n).astype(f32)
    lanes = lax.broadcasted_iota(jnp.int32, (n, n), 1)
    rows = lax.broadcasted_iota(jnp.int32, (n, n), 0)
    want4 = jnp.sum(jnp.where(owner4 == lanes, rem4, 0.0), axis=0, keepdims=True)
    owner5_row = order5_ref[...] // n
    owner5 = column(owner5_row)
    rem5 = column(order5_ref[...] % n).astype(f32)
    earlier = jnp.where((owner5 == owner5_row) & (rows < lanes), 1.0, 0.0)
    rank_row = jnp.sum(earlier, axis=0, keepdims=True).astype(jnp.int32)
    rank = column(rank_row)
    mine = (owner5 == lanes // 4) & (rank == x)
    want5 = jnp.sum(jnp.where(mine, rem5, 0.0), axis=0, keepdims=True)
    out_ref[...] = jnp.concatenate([want4, want5], axis=0).astype(jnp.int32)
    slot_ref[...] = owner5_row * 4 + rank_row


def pick_kernel(index_ref, table_ref, out_ref):
    out_ref[...] = dot(one_hot(column(index_ref[...]), table_ref.shape[0]), table_ref[...]).astype(
        bf16
    )


def norm4_kernel(order4_ref, arrived_ref, gain_ref, rows_ref, normed_ref):
    n = arrived_ref.shape[0]
    rows = dot(one_hot(column(order4_ref[...] // n), n), arrived_ref[...]).astype(bf16)
    rows_ref[...] = rows
    normed_ref[...] = layer_norm(rows, gain_ref[...])


def attend(heads, k_ref, qt_ref, vt_ref, at_ref, s_ref, chunk=512):
    width = heads * HEAD
    queries = qt_ref.shape[1]
    keys = k_ref.shape[0]
    row_head = lax.broadcasted_iota(jnp.int32, (width, queries), 0) // HEAD

    def of_head(head):
        q = qt_ref[...]
        return jnp.where(row_head == head, q, jnp.zeros_like(q))

    def score(q_head, slot, c, top):
        s = dot(k_ref[c * chunk : (c + 1) * chunk, :], q_head)
        s_ref[slot, c * chunk : (c + 1) * chunk, :] = s
        return jnp.maximum(top, jnp.max(s.reshape(chunk // 8, 8, queries), axis=0))

    def low():
        return jnp.full((8, queries), -jnp.inf, f32)

    def step(head, slot, peak, more):
        mixed = jnp.zeros((2 * HEAD, queries), f32)
        top = low()
        q_next = of_head(head + 1) if more else None
        for c in range(keys // chunk):
            if more:
                top = score(q_next, 1 - slot, c, top)
            p = jnp.exp(s_ref[slot, c * chunk : (c + 1) * chunk, :] - peak).astype(bf16)
            mixed = mixed + dot(vt_ref[head, :, c * chunk : (c + 1) * chunk], p)
        at_ref[head] = (mixed[:HEAD] / mixed[HEAD:]).astype(bf16)
        return jnp.max(top, axis=0, keepdims=True)

    top = low()
    q_first = of_head(0)
    for c in range(keys // chunk):
        top = score(q_first, 0, c, top)
    peak = jnp.max(top, axis=0, keepdims=True)

    def pair(i, peak):
        peak = step(2 * i, 0, peak, True)
        return step(2 * i + 1, 1, peak, True)

    peak = lax.fori_loop(0, heads // 2 - 1, pair, peak)
    peak = step(heads - 2, 0, peak, True)
    step(heads - 1, 1, peak, False)
    return jnp.transpose(at_ref[...].reshape(width, queries))


def attend_scratch(heads, queries, keys):
    width = heads * HEAD
    return [
        pltpu.VMEM((keys, width), bf16),
        pltpu.VMEM((width, queries), bf16),
        pltpu.VMEM((heads, 2 * HEAD, keys), bf16),
        pltpu.VMEM((heads, HEAD, queries), bf16),
        pltpu.VMEM((2, keys, queries), f32),
    ]


def load_values(vt_ref, values, heads):
    keys = values.shape[0]
    vt_ref[:, :HEAD, :] = jnp.transpose(values).reshape(heads, HEAD, keys)
    vt_ref[:, HEAD:, :] = jnp.ones((heads, HEAD, keys), bf16)


SCALE = 1.0 / math.sqrt(HEAD)


def fine_kernel(own_ref, other_ref, rows_ref, qkv_ref, proj_ref, out_ref, k, qt, vt, at, s):
    n = own_ref.shape[0]
    own, other = own_ref[...], other_ref[...]
    query = dot(own, qkv_ref[0]).astype(bf16) * bf16(SCALE)
    qt[...] = jnp.transpose(query)
    k[:n] = dot(own, qkv_ref[1]).astype(bf16)
    k[n:] = dot(other, qkv_ref[1]).astype(bf16)
    values = jnp.concatenate([dot(own, qkv_ref[2]), dot(other, qkv_ref[2])], axis=0)
    load_values(vt, values.astype(bf16), H4)
    attended = attend(H4, k, qt, vt, at, s)
    out_ref[...] = (rows_ref[...].astype(f32) + dot(attended, proj_ref[...])).astype(bf16)


def coarse_kernel(q_ref, own_ref, other_ref, proj_ref, out_ref, k, qt, vt, at, s):
    n, width = q_ref.shape
    qt[...] = jnp.transpose(q_ref[...] * bf16(SCALE))
    k[:n] = own_ref[:, :width]
    k[n:] = other_ref[:, :width]
    values = jnp.concatenate([own_ref[:, width:], other_ref[:, width:]], axis=0)
    load_values(vt, values, width // HEAD)
    attended = attend(width // HEAD, k, qt, vt, at, s)
    terms = dot(attended, proj_ref[...]).astype(bf16)
    parts = out_ref.shape[0]
    for g in range(parts):
        out_ref[g] = terms[:, g * width : (g + 1) * width]


def pool_kernel(fine_ref, weight_ref, child_ref, index_ref, base_ref, out_ref):
    total = fine_ref.shape[0]
    points = child_ref.shape[1]
    width = weight_ref.shape[1]
    lifted = dot(fine_ref[...], weight_ref[...])
    start_row = child_ref[0:1, :] - base_ref[0]
    start = column(start_row)
    rows = lax.broadcasted_iota(jnp.int32, (total, points), 0)
    first = jnp.where(start_row == rows, 1.0, 0.0).astype(bf16)
    opens = dot(first, jnp.ones((points, width), bf16))

    def ahead(block, k):
        return jnp.concatenate([block[k:], jnp.ones((k, width), f32)], axis=0)

    cut = ahead(opens, 1)
    best = lifted
    reach = 1
    while reach < KIDS:
        best = jnp.where(cut > 0.0, best, jnp.maximum(best, ahead(best, reach)))
        cut = jnp.maximum(cut, ahead(cut, reach))
        reach *= 2
    pooled_rows = jax.nn.gelu(best, approximate=True).astype(bf16)
    pooled = dot(one_hot(start, total), pooled_rows).astype(bf16)
    out_ref[...] = dot(one_hot(column(index_ref[...]), points), pooled).astype(bf16)


def norm5_kernel(slot_ref, parts_ref, own_ref, gain_ref, qkv_ref, q_ref, kv_ref, cols_ref):
    n = slot_ref.shape[1]
    width = own_ref.shape[1]
    pick = one_hot(column(slot_ref[...]), n)
    rows = jnp.concatenate(
        [dot(pick, parts_ref[g]).astype(bf16) for g in range(parts_ref.shape[0])], axis=1
    )
    cols_ref[...] = dot(pick, own_ref[...]).astype(bf16)
    normed = layer_norm(rows, gain_ref[...])
    q_ref[...] = dot(normed, qkv_ref[0]).astype(bf16)
    kv_ref[:, :width] = dot(normed, qkv_ref[1]).astype(bf16)
    kv_ref[:, width:] = dot(normed, qkv_ref[2]).astype(bf16)


def sum_kernel(cols_ref, parts_ref, out_ref):
    total = cols_ref[...].astype(f32)
    summed = parts_ref[0].astype(f32)
    for g in range(1, parts_ref.shape[0]):
        summed = summed + parts_ref[g].astype(f32)
    out_ref[...] = (total + summed).astype(bf16)


def shape(dims, dtype=bf16):
    return jax.ShapeDtypeStruct(dims, dtype)


def exchange(block, axes):
    return lax.all_to_all(block, axes, split_axis=0, concat_axis=0, tiled=True)


def local(
    feats4, order4, gain4, qkv4, proj4, pool_weight, child5, mask5, order5, gain5, qkv5, proj5
):
    n = feats4.shape[0]
    nz = lax.axis_size("z")
    plane = lax.axis_size("y") * lax.axis_size("c") * lax.axis_size("x")
    nx = lax.axis_size("x")
    pts_count = nz * lax.axis_size("y") * lax.axis_size("c")
    pts_index = lax.axis_index(PTS)
    grp_index = lax.axis_index("x")
    order4_row = order4.reshape(1, n)

    wanted, slots = pl.pallas_call(
        request_kernel,
        out_shape=[shape((2, n), jnp.int32), shape((1, n), jnp.int32)],
        compiler_params=params(),
        name="request",
    )(order4_row, order5.reshape(1, n))
    by_z = exchange(wanted.reshape(2, nz, plane).transpose(1, 0, 2), ("z",))
    by_plane = exchange(by_z.transpose(2, 1, 0), PLANE)
    asked = by_plane.transpose(1, 2, 0).reshape(2, n)

    outgoing = pl.pallas_call(
        pick_kernel, out_shape=shape((n, C4)), compiler_params=params(), name="pick4"
    )(asked[0:1], feats4)
    arrived = exchange(outgoing, ALL)
    curve_rows, normed4 = pl.pallas_call(
        norm4_kernel,
        out_shape=[shape((n, C4)), shape((n, C4))],
        compiler_params=params(),
        name="norm4",
    )(order4_row, arrived, gain4.reshape(1, C4))
    other4 = lax.ppermute(normed4, "x", [(i, i ^ 1) for i in range(nx)])
    fine_out = pl.pallas_call(
        fine_kernel,
        out_shape=shape((n, C4)),
        scratch_shapes=attend_scratch(H4, n, 2 * n),
        compiler_params=params(),
        name="attend4",
    )(normed4, other4, curve_rows, qkv4, proj4)

    width = C5 // nx
    fine_all = exchange(jnp.broadcast_to(fine_out[None], (nx, n, C4)), "x").reshape(nx * n, C4)
    base = (pts_index * (nx * n)).reshape(1).astype(jnp.int32)
    own_weight = lax.dynamic_slice_in_dim(pool_weight, grp_index * width, width, 1)
    smem = pl.BlockSpec(memory_space=pltpu.SMEM)
    vmem = pl.BlockSpec(memory_space=pltpu.VMEM)
    pooled = pl.pallas_call(
        pool_kernel,
        out_shape=shape((n, width)),
        in_specs=[vmem, vmem, vmem, vmem, smem],
        compiler_params=params(),
        name="pool",
    )(fine_all, own_weight, child5.T, asked[1:2], base)
    own_part = exchange(pooled.reshape(pts_count, n // pts_count, width), PTS).reshape(n, width)
    parts = exchange(jnp.broadcast_to(own_part[None], (nx, n, width)), "x")
    query5, kv5, own_columns = pl.pallas_call(
        norm5_kernel,
        out_shape=[shape((n, width)), shape((n, 2 * width)), shape((n, width))],
        compiler_params=params(),
        name="norm5",
    )(slots, parts, own_part, gain5.reshape(1, C5), qkv5)
    other5 = lax.ppermute(kv5, "c", [(0, 1), (1, 0)])
    terms = pl.pallas_call(
        coarse_kernel,
        out_shape=shape((nx, n, width)),
        scratch_shapes=attend_scratch(width // HEAD, n, 2 * n),
        compiler_params=params(),
        name="attend5",
    )(query5, kv5, other5, proj5)
    summed = exchange(terms, "x")
    coarse_out = pl.pallas_call(
        sum_kernel, out_shape=shape((n, width)), compiler_params=params(), name="add5"
    )(own_columns, summed)
    return (fine_out, coarse_out)


def solution(mesh):
    pts, grp = mesh.devices.shape
    inner = Mesh(mesh.devices.reshape(pts // 8, 4, 2, grp), ALL)
    in_specs = (
        P(ALL, None),
        P(ALL),
        P(),
        P(),
        P(),
        P(),
        P(PTS, None),
        P(PTS, None),
        P(PTS),
        P(),
        P(None, None, "x"),
        P("x", None),
    )
    out_specs = (P(ALL, None), P(PTS, "x"))
    return jax.shard_map(local, mesh=inner, in_specs=in_specs, out_specs=out_specs, check_vma=False)
```

```python
import functools
import math

import jax
import jax.numpy as jnp
from jax import lax
from jax.experimental import pallas as pl
from jax.experimental.pallas import tpu as pltpu
from jax.sharding import Mesh
from jax.sharding import PartitionSpec as P

C4 = 256
H4 = 16
C5 = 512
H5 = 32
HEAD = 16
KIDS = 8

epsilon = 1e-05
f32 = jnp.float32
bf16 = jnp.bfloat16

PTS = ("z", "y", "c")
PLANE = ("y", "c", "x")
ALL = ("z", "y", "c", "x")


def dot(a, b):
    return jnp.dot(a, b, preferred_element_type=f32)


def column(row):
    return jnp.transpose(jnp.broadcast_to(row, (8, row.shape[1])))[:, :1]


def one_hot(col, width):
    lanes = lax.broadcasted_iota(jnp.int32, (col.shape[0], width), 1)
    return jnp.where(col == lanes, 1.0, 0.0).astype(bf16)


def layer_norm(rows_in, norm_gain):
    values = rows_in.astype(f32)
    center = values - jnp.mean(values, axis=-1, keepdims=True)
    spread = jnp.mean(center * center, axis=-1, keepdims=True)
    return (center * lax.rsqrt(spread + epsilon) * norm_gain).astype(bf16)


def fetch(pairs, sems):
    copies = [pltpu.make_async_copy(a, b, sems.at[i]) for i, (a, b) in enumerate(pairs)]
    for copy in copies:
        copy.start()
    return copies


def request_kernel(planes, order4_hbm, order5_hbm, out_ref, owner_ref, slot_ref, o4, o5, sems):
    for copy in fetch([(order4_hbm, o4), (order5_hbm, o5)], sems):
        copy.wait()
    n = o4.shape[1]
    nz, nx = out_ref.shape[0], lax.axis_size("x")
    x = lax.axis_index("x")
    owner4, owner5 = o4[...] // n, o5[...] // n
    owner_ref[...] = owner4
    owner5_col = column(owner5)
    lanes = lax.broadcasted_iota(jnp.int32, (n, n), 1)
    rows = lax.broadcasted_iota(jnp.int32, (n, n), 0)
    earlier = jnp.where((owner5_col == owner5) & (rows < lanes), 1.0, 0.0)
    rank = jnp.sum(earlier, axis=0, keepdims=True).astype(jnp.int32)
    per_z = planes // nx
    slot_ref[...] = ((owner5 % per_z) * nz + owner5 // per_z) * nx + rank

    lane = lax.broadcasted_iota(jnp.int32, (n, planes), 1)
    zs = lax.broadcasted_iota(jnp.int32, (nz, n), 0)

    def table(z_of, u_hit, row):
        z_hit = jnp.where(zs == z_of, 1.0, 0.0).astype(bf16)
        low = jnp.where(u_hit, (row % 256).astype(f32), 0.0).astype(bf16)
        high = jnp.where(u_hit, (row // 256).astype(f32), 0.0).astype(bf16)
        return dot(z_hit, low) + 256.0 * dot(z_hit, high)

    want4 = table(owner4 // planes, column(owner4 % planes) == lane, column(o4[...] % n))
    hit5 = (column(owner5 % per_z) == lane // nx) & (column(rank) == x)
    want5 = table(owner5 // per_z, hit5, column(o5[...] % n))
    out_ref[:, 0, :] = want4.astype(jnp.int32)
    out_ref[:, 1, :] = want5.astype(jnp.int32)


def pick_of(asked_ref, which, width):
    asked = asked_ref[:, which, :]
    cols = [asked[:, z : z + 1] for z in range(asked.shape[1])]
    return jnp.concatenate([one_hot(col, width) for col in cols], axis=0)


def pick_kernel(asked_ref, table_ref, out_ref):
    out_ref[...] = dot(pick_of(asked_ref, 0, table_ref.shape[0]), table_ref[...]).astype(bf16)


def norm4_kernel(owner_ref, arrived_ref, gain_hbm, rows_ref, normed_ref, gain, sems):
    copies = fetch([(gain_hbm, gain)], sems)
    n = arrived_ref.shape[0]
    rows = dot(one_hot(column(owner_ref[...]), n), arrived_ref[...]).astype(bf16)
    rows_ref[...] = rows
    copies[0].wait()
    normed_ref[...] = layer_norm(rows, gain[...])


def attend(heads, k_ref, qt_ref, vt_ref, s_ref, finish, before=None, chunk=512):
    width = heads * HEAD
    queries = qt_ref.shape[1]
    keys = k_ref.shape[0]
    row_head = lax.broadcasted_iota(jnp.int32, (width, queries), 0) // HEAD

    def of_head(head):
        q = qt_ref[...]
        return jnp.where(row_head == head, q, jnp.zeros_like(q))

    def score(q_head, slot, c, top):
        s = dot(k_ref[c * chunk : (c + 1) * chunk, :], q_head)
        s_ref[slot, c * chunk : (c + 1) * chunk, :] = s
        return jnp.maximum(top, jnp.max(s.reshape(chunk // 8, 8, queries), axis=0))

    def low():
        return jnp.full((8, queries), -jnp.inf, f32)

    def step(head, slot, peak, more):
        if before is None:
            mixed = jnp.zeros((2 * HEAD, queries), f32)
        else:
            earlier, mixed = before(head)
            peak = jnp.maximum(peak, earlier)
            mixed = mixed * jnp.exp(earlier - peak)
        top = low()
        q_next = of_head(head + 1) if more else None
        for c in range(keys // chunk):
            if more:
                top = score(q_next, 1 - slot, c, top)
            p = jnp.exp(s_ref[slot, c * chunk : (c + 1) * chunk, :] - peak).astype(bf16)
            mixed = mixed + dot(vt_ref[head, :, c * chunk : (c + 1) * chunk], p)
        finish(head, peak, mixed)
        return jnp.max(top, axis=0, keepdims=True)

    top = low()
    q_first = of_head(0)
    for c in range(keys // chunk):
        top = score(q_first, 0, c, top)
    peak = jnp.max(top, axis=0, keepdims=True)

    def pair(i, peak):
        peak = step(2 * i, 0, peak, True)
        return step(2 * i + 1, 1, peak, True)

    peak = lax.fori_loop(0, heads // 2 - 1, pair, peak)
    peak = step(heads - 2, 0, peak, True)
    step(heads - 1, 1, peak, False)


def divide(at_ref):
    def finish(head, peak, mixed):
        at_ref[head] = (mixed[:HEAD] / mixed[HEAD:]).astype(bf16)

    return finish


def joined(at_ref):
    heads, size, queries = at_ref.shape
    return jnp.transpose(at_ref[...].reshape(heads * size, queries))


def attend_scratch(heads, queries, keys):
    width = heads * HEAD
    return [
        pltpu.VMEM((keys, width), bf16),
        pltpu.VMEM((heads, 2 * HEAD, keys), bf16),
        pltpu.VMEM((2, keys, queries), f32),
    ]


def load_values(vt_ref, values, heads):
    keys = values.shape[0]
    vt_ref[:, :HEAD, :] = jnp.transpose(values).reshape(heads, HEAD, keys)
    vt_ref[:, HEAD:, :] = jnp.ones((heads, HEAD, keys), bf16)


SCALE = 1.0 / math.sqrt(HEAD)


def own_kernel(own_ref, qkv_ref, qt_ref, peak_ref, mixed_ref, k, vt, s):
    own = own_ref[...]
    qt_ref[...] = jnp.transpose(dot(own, qkv_ref[0]).astype(bf16) * bf16(SCALE))
    k[...] = dot(own, qkv_ref[1]).astype(bf16)
    load_values(vt, dot(own, qkv_ref[2]).astype(bf16), H4)

    def finish(head, peak, mixed):
        peak_ref[head] = peak
        mixed_ref[head] = mixed

    attend(H4, k, qt_ref, vt, s, finish)


def other_kernel(
    other_ref,
    qkv_ref,
    qt_ref,
    peak_ref,
    mixed_ref,
    rows_ref,
    proj_ref,
    weight_ref,
    child_ref,
    out_ref,
    parts_ref,
    k,
    vt,
    s,
    at,
):
    other = other_ref[...]
    k[...] = dot(other, qkv_ref[1]).astype(bf16)
    load_values(vt, dot(other, qkv_ref[2]).astype(bf16), H4)
    attend(H4, k, qt_ref, vt, s, divide(at), lambda head: (peak_ref[head], mixed_ref[head]))
    fine = (rows_ref[...].astype(f32) + dot(joined(at), proj_ref[...])).astype(bf16)
    out_ref[...] = fine
    pool_own(fine, weight_ref, child_ref, parts_ref)


def coarse_kernel(q_ref, both_ref, proj_ref, out_ref, k, vt, s, qt, at):
    n, width = q_ref.shape
    qt[...] = jnp.transpose(q_ref[...] * bf16(SCALE))
    k[...] = both_ref[:, :width]
    values = both_ref[:, width:]
    load_values(vt, values, width // HEAD)
    attend(width // HEAD, k, qt, vt, s, divide(at))
    terms = dot(joined(at), proj_ref[...]).astype(bf16)
    parts = out_ref.shape[0]
    for g in range(parts):
        out_ref[g] = terms[:, g * width : (g + 1) * width]


EDGE = 16


def gelu(values):
    return jax.nn.gelu(values, approximate=True).astype(bf16)


def three_terms(value):
    first = value.astype(bf16).astype(f32)
    second = (value - first).astype(bf16).astype(f32)
    return [first, second, value - first - second]


def run_starts(child_ref, n):
    nx = lax.axis_size("x")
    return child_ref[0:1, :] - lax.axis_index(PTS) * (nx * n)


def pool_own(fine, weight_ref, child_ref, parts_ref):
    n = fine.shape[0]
    points = child_ref.shape[1]
    groups, _, width = parts_ref.shape
    start_row = run_starts(child_ref, n) - lax.axis_index("x") * n
    start = column(start_row)
    rows = lax.broadcasted_iota(jnp.int32, (n, points), 0)
    first = jnp.where(start_row == rows, 1.0, 0.0).astype(bf16)
    opens = dot(first, jnp.ones((points, width), bf16))
    place = one_hot(start, n)
    last = jnp.max(
        jnp.where(start_row < n, start_row.astype(f32), -1.0), axis=1, keepdims=True
    ).astype(jnp.int32)
    tail = KIDS
    leaving = lax.broadcasted_iota(jnp.int32, (tail, width), 0) + (n - tail) >= last
    edge_row = lax.broadcasted_iota(jnp.int32, (EDGE, width), 0)

    def ahead(block, k):
        return jnp.concatenate([block[k:], jnp.ones((k, width), f32)], axis=0)

    cut = ahead(opens, 1)
    cuts = []
    reach = 1
    while reach < KIDS:
        cuts.append((reach, cut > 0.0))
        cut = jnp.maximum(cut, ahead(cut, reach))
        reach *= 2
    for g in range(groups):
        best = dot(fine, weight_ref[:, g * width : (g + 1) * width])
        lifted_tail = best[n - tail :]
        for reach, ends in cuts:
            best = jnp.where(ends, best, jnp.maximum(best, ahead(best, reach)))
        parts_ref[g, :points, :] = dot(place, gelu(best)).astype(bf16)
        head = jnp.max(jnp.where(leaving, lifted_tail, -jnp.inf), axis=0, keepdims=True)
        edge = jnp.zeros((EDGE, width), f32)
        for at, value in ((0, head), (8, best[0:1])):
            for i, term in enumerate(three_terms(value)):
                edge = jnp.where(edge_row == at + i, term, edge)
        parts_ref[g, points:, :] = edge.astype(bf16)


def pool_kernel(parts_ref, child_ref, asked_ref, out_ref):
    groups = parts_ref.shape[0]
    points = child_ref.shape[1]
    n, width = out_ref.shape
    start_row = run_starts(child_ref, n)
    point = lax.broadcasted_iota(jnp.int32, (points, width), 0)
    pooled = parts_ref[0, :points, :].astype(f32)
    for g in range(1, groups):
        pooled = pooled + parts_ref[g, :points, :].astype(f32)

    def edge(g, at):
        block = parts_ref[g, points:, :].astype(f32)
        return block[at : at + 1] + block[at + 1 : at + 2] + block[at + 2 : at + 3]

    def count(hits):
        return jnp.sum(jnp.where(hits, 1.0, 0.0), axis=1, keepdims=True).astype(jnp.int32)

    for g in range(1, groups):
        whole = gelu(jnp.maximum(edge(g - 1, 0), edge(g, 8))).astype(f32)
        crossing = count(start_row < g * n) - 1
        crossing = jnp.where(count(start_row == g * n) > 0, -1, crossing)
        pooled = jnp.where(point == crossing, whole, pooled)
    out_ref[...] = dot(pick_of(asked_ref, 1, points), pooled.astype(bf16)).astype(bf16)


def norm5_kernel(
    slot_ref, parts_ref, gain_hbm, qkv_ref, q_ref, kv_ref, cols_ref, gain, sems
):
    copies = fetch([(gain_hbm, gain)], sems)
    n = slot_ref.shape[1]
    groups, width = parts_ref.shape[1], parts_ref.shape[3]
    pick = one_hot(column(slot_ref[...]), n)
    parts = [parts_ref[:, g].reshape(n, width) for g in range(groups)]
    own = parts_ref[:, pl.ds(lax.axis_index("x"), 1)].reshape(n, width)
    picked = dot(pick, jnp.concatenate(parts + [own], axis=1)).astype(bf16)
    rows = picked[:, : groups * width]
    cols_ref[...] = picked[:, groups * width :]
    copies[0].wait()
    normed = layer_norm(rows, gain[...])
    q_ref[...] = dot(normed, qkv_ref[0]).astype(bf16)
    kv_ref[:, :width] = dot(normed, qkv_ref[1]).astype(bf16)
    kv_ref[:, width:] = dot(normed, qkv_ref[2]).astype(bf16)


def sum_kernel(cols_ref, parts_ref, out_ref):
    total = cols_ref[...].astype(f32)
    summed = parts_ref[0].astype(f32)
    for g in range(1, parts_ref.shape[0]):
        summed = summed + parts_ref[g].astype(f32)
    out_ref[...] = (total + summed).astype(bf16)


def shape(dims, dtype=bf16):
    return jax.ShapeDtypeStruct(dims, dtype)


def exchange(block, axes):
    return lax.all_to_all(block, axes, split_axis=0, concat_axis=0, tiled=True)


VMEM = pl.BlockSpec(memory_space=pltpu.VMEM)
HBM = pl.BlockSpec(memory_space=pltpu.HBM)
DMA = pltpu.SemaphoreType.DMA


def kernel(body, name, out_shape, scratch=(), in_specs=None, flops=0):
    extra = {} if in_specs is None else {"in_specs": in_specs}
    if flops:
        extra["cost_estimate"] = pl.CostEstimate(
            flops=flops, bytes_accessed=1 << 20, transcendentals=0
        )
    return pl.pallas_call(
        body,
        out_shape=out_shape,
        scratch_shapes=list(scratch),
        compiler_params=pltpu.CompilerParams(vmem_limit_bytes=48 << 20),
        name=name,
        **extra,
    )


def local(
    feats4, order4, gain4, qkv4, proj4, pool_weight, child5, mask5, order5, gain5, qkv5, proj5
):
    n = feats4.shape[0]
    nz = lax.axis_size("z")
    planes = lax.axis_size("y") * lax.axis_size("c") * lax.axis_size("x")
    nx = lax.axis_size("x")
    pts_count = nz * planes // nx

    wanted, owner4, slot5 = kernel(
        functools.partial(request_kernel, planes),
        "request",
        [shape((nz, 2, planes), jnp.int32), shape((1, n), jnp.int32), shape((1, n), jnp.int32)],
        [pltpu.VMEM((1, n), jnp.int32), pltpu.VMEM((1, n), jnp.int32), DMA((2,))],
        [HBM, HBM],
    )(order4.reshape(1, n), order5.reshape(1, n))
    asked = exchange(exchange(wanted, ("z",)).transpose(2, 1, 0), PLANE)

    outgoing = kernel(pick_kernel, "pick4", shape((n, C4)))(asked, feats4)
    arrived = exchange(outgoing.reshape(n, 2, C4 // 2), ALL).reshape(n, C4)
    curve_rows, normed4 = kernel(
        norm4_kernel,
        "norm4",
        [shape((n, C4)), shape((n, C4))],
        [pltpu.VMEM((1, C4), f32), DMA((1,))],
        [VMEM, VMEM, HBM],
    )(owner4, arrived, gain4.reshape(1, C4))
    other4 = lax.ppermute(normed4, "x", [(i, i ^ 1) for i in range(nx)])
    half = 4 * n * n * C4 * H4
    qt4, peak4, mixed4 = kernel(
        own_kernel,
        "attend4_own",
        [shape((C4, n)), shape((H4, 1, n), f32), shape((H4, 2 * HEAD, n), f32)],
        attend_scratch(H4, n, n),
        flops=half,
    )(normed4, qkv4)
    child_rows = child5.T
    width = C5 // nx
    fine_out, parts4 = kernel(
        other_kernel,
        "attend4_other",
        [shape((n, C4)), shape((nx, n + EDGE, width))],
        attend_scratch(H4, n, n) + [pltpu.VMEM((H4, HEAD, n), bf16)],
        flops=half,
    )(other4, qkv4, qt4, peak4, mixed4, curve_rows, proj4, pool_weight, child_rows)

    pooled = kernel(pool_kernel, "pool", shape((n, width)))(
        exchange(parts4, "x"), child_rows, asked
    )
    by_z = exchange(pooled.reshape(nz, n // nz, width), ("z",))
    by_z = by_z.reshape(nz, planes // nx, n // pts_count, width).transpose(1, 0, 2, 3)
    copies = jnp.broadcast_to(
        by_z.reshape(planes // nx, 1, n * nx // planes, width),
        (planes // nx, nx, n * nx // planes, width),
    )
    parts5 = exchange(copies.reshape(planes, n * nx // planes, width), PLANE)
    parts5 = parts5.reshape(copies.shape)
    query5, kv5, own_columns = kernel(
        norm5_kernel,
        "norm5",
        [shape((n, width)), shape((n, 2 * width)), shape((n, width))],
        [pltpu.VMEM((1, C5), f32), DMA((1,))],
        [VMEM, VMEM, HBM, VMEM],
    )(slot5, parts5, gain5.reshape(1, C5), qkv5)
    both5 = lax.all_gather(kv5, "c", axis=0, tiled=True)
    terms = kernel(
        coarse_kernel,
        "attend5",
        shape((nx, n, width)),
        attend_scratch(width // HEAD, n, 2 * n)
        + [pltpu.VMEM((width, n), bf16), pltpu.VMEM((width // HEAD, HEAD, n), bf16)],
    )(query5, both5, proj5)
    coarse_out = kernel(sum_kernel, "add5", shape((n, width)))(own_columns, exchange(terms, "x"))
    return (fine_out, coarse_out)


def solution(mesh):
    pts, grp = mesh.devices.shape
    inner = Mesh(mesh.devices.reshape(pts // 8, 4, 2, grp), ALL)
    in_specs = (
        P(ALL, None),
        P(ALL),
        P(),
        P(),
        P(),
        P(),
        P(PTS, None),
        P(PTS, None),
        P(PTS),
        P(),
        P(None, None, "x"),
        P("x", None),
    )
    out_specs = (P(ALL, None), P(PTS, "x"))
    return jax.shard_map(local, mesh=inner, in_specs=in_specs, out_specs=out_specs, check_vma=False)
```

```python
import functools
import math

import jax
import jax.numpy as jnp
from jax import lax
from jax.experimental import pallas as pl
from jax.experimental.pallas import tpu as pltpu
from jax.sharding import Mesh
from jax.sharding import PartitionSpec as P

C4 = 256
H4 = 16
C5 = 512
H5 = 32
HEAD = 16
KIDS = 8

epsilon = 1e-05
f32 = jnp.float32
bf16 = jnp.bfloat16

PTS = ("z", "y", "c")
PLANE = ("y", "c", "x")
CHIPS = ("z", "y", "x")
ALL = ("z", "y", "c", "x")


def dot(a, b):
    return jnp.dot(a, b, preferred_element_type=f32)


def column(row):
    return jnp.transpose(jnp.broadcast_to(row, (8, row.shape[1])))[:, :1]


def columns(*rows):
    n = rows[0].shape[1]
    fill = [jnp.zeros((8 - len(rows), n), jnp.int32)] if len(rows) < 8 else []
    block = jnp.transpose(jnp.concatenate(list(rows) + fill, axis=0))
    return [block[:, i : i + 1] for i in range(len(rows))]


def one_hot(col, width):
    lanes = lax.broadcasted_iota(jnp.int32, (col.shape[0], width), 1)
    return jnp.where(col == lanes, 1.0, 0.0).astype(bf16)


def layer_norm(rows_in, norm_gain):
    values = rows_in.astype(f32)
    center = values - jnp.mean(values, axis=-1, keepdims=True)
    spread = jnp.mean(center * center, axis=-1, keepdims=True)
    return (center * lax.rsqrt(spread + epsilon) * norm_gain).astype(bf16)


def fetch(pairs, sems):
    copies = [pltpu.make_async_copy(a, b, sems.at[i]) for i, (a, b) in enumerate(pairs)]
    for copy in copies:
        copy.start()
    return copies


def request_kernel(planes, orders_ref, out_ref, owner_ref, slot_ref):
    o4, o5 = orders_ref[0:1, :], orders_ref[1:2, :]
    n = o4.shape[1]
    nz, nx = out_ref.shape[0], lax.axis_size("x")
    x = lax.axis_index("x")
    owner4, owner5 = o4 // n, o5 // n
    ny, half, per_z = planes // (2 * nx), planes // 2, planes // nx
    u = owner4 % planes
    lane4 = u // nx % 2 * half + u // (2 * nx) * nx + u % nx
    owner_ref[...] = u // nx % 2 * (n // 2) + owner4 // planes * half + lane4 % half
    of_pts = owner5 % per_z
    pair5 = of_pts % 2 * ny + of_pts // 2
    lane4_col, row4_col, owner5_col, pair5_col, row5_col = columns(
        lane4, o4 % n, owner5, pair5, o5 % n
    )

    lanes = lax.broadcasted_iota(jnp.int32, (n, n), 1)
    rows = lax.broadcasted_iota(jnp.int32, (n, n), 0)
    earlier = jnp.where((owner5_col == owner5) & (rows < lanes), 1.0, 0.0)
    rank = jnp.sum(earlier, axis=0, keepdims=True).astype(jnp.int32)
    slot_ref[...] = ((owner5 % per_z) * nz + owner5 // per_z) * nx + rank

    lane = lax.broadcasted_iota(jnp.int32, (n, planes), 1)
    zs = lax.broadcasted_iota(jnp.int32, (nz, n), 0)

    def table(z_hit, u_hit, row):
        low = jnp.where(u_hit, (row % 256).astype(f32), 0.0)
        high = jnp.where(u_hit, (row // 256).astype(f32), 0.0)
        both = dot(
            jnp.where(z_hit, 1.0, 0.0).astype(bf16),
            jnp.concatenate([low, high], axis=1).astype(bf16),
        )
        return (both[:, :planes] + 256.0 * both[:, planes:]).astype(jnp.int32)

    want4 = table(zs == owner4 // planes, lane4_col == lane, row4_col)
    own_rank = (zs == owner5 // per_z) & (rank == x)
    want5 = table(own_rank, pair5_col == lane // nx, row5_col)
    for c in range(2):
        out_ref[:, c, :] = want4[:, c * half : (c + 1) * half]
        out_ref[:, 2 + c, :] = want5[:, c * half : (c + 1) * half]


def picks(cols, width):
    return jnp.concatenate([one_hot(cols[:, i : i + 1], width) for i in range(cols.shape[1])], axis=0)


def pick_kernel(asked_ref, table_ref, out_ref):
    nz = asked_ref.shape[1] // 4
    n, width = table_ref.shape[0] // 2, table_ref.shape[1]
    for c in range(2):
        pick = picks(asked_ref[:, c * nz : (c + 1) * nz], n)
        out_ref[:, c * width : (c + 1) * width] = dot(
            pick, table_ref[c * n : (c + 1) * n, :]
        ).astype(bf16)


def prepare_kernel(
    owner_ref,
    slot_ref,
    asked_ref,
    child_ref,
    gain_ref,
    pick4_ref,
    pick5_ref,
    want5_ref,
    place_ref,
    ends_ref,
    gain_out_ref,
):
    gain_out_ref[...] = gain_ref[...]
    n = owner_ref.shape[1]
    points = child_ref.shape[1]
    pick4_ref[...] = one_hot(column(owner_ref[...]), n)
    pick5_ref[...] = one_hot(column(slot_ref[...]), n)

    start_row = run_starts(child_ref, n)
    room = place_ref.shape[0]
    at = lax.broadcasted_iota(jnp.int32, (1, points), 1)
    for g in range(want5_ref.shape[1] // room):
        before = count(start_row < g * n)
        at = jnp.where(start_row // n == g, at - before + g * room, at)
    nz = asked_ref.shape[1] // 4
    asked5 = jnp.where(
        lax.axis_index("c") == 0, asked_ref[:, 2 * nz : 3 * nz], asked_ref[:, 3 * nz :]
    )
    wanted = picks(asked5, points).astype(f32)
    spot = jnp.sum(wanted * at.astype(f32), axis=1, keepdims=True).astype(jnp.int32)
    want5_ref[...] = one_hot(spot, want5_ref.shape[1])

    own_row = own_starts(child_ref, n)
    own = column(own_row)
    lanes = lax.broadcasted_iota(jnp.int32, (points, n), 1)
    opened = jnp.where((own >= 0) & (own <= lanes), 1.0, 0.0)
    number = jnp.sum(opened, axis=0, keepdims=True).astype(jnp.int32) - 1
    opens_here = jnp.sum(jnp.where(own == lanes, 1.0, 0.0), axis=0, keepdims=True)
    spots = lax.broadcasted_iota(jnp.int32, (room, n), 0)
    place_ref[...] = jnp.where((spots == number) & (opens_here > 0.0), 1.0, 0.0).astype(bf16)

    rows = lax.broadcasted_iota(jnp.int32, (n, points), 0)
    first = jnp.where(own_row == rows, 1.0, 0.0).astype(bf16)
    opens = dot(first, jnp.ones((points, ends_ref.shape[2]), bf16))
    cut = ahead(opens, 1, 1.0)
    for i in range(ends_ref.shape[0]):
        ends_ref[i] = cut
        cut = jnp.maximum(cut, ahead(cut, 1 << i, 1.0))


def norm4_kernel(pick_ref, arrived_ref, gain_ref, rows_ref, normed_ref):
    width = rows_ref.shape[1]
    arrived = jnp.concatenate([arrived_ref[:, :width], arrived_ref[:, width:]], axis=0)
    rows = dot(pick_ref[...], arrived).astype(bf16)
    rows_ref[...] = rows
    normed_ref[...] = layer_norm(rows, gain_ref[...])


def attend(heads, k_ref, qt_ref, vt_ref, s_ref, finish, before=None, chunk=512):
    width = heads * HEAD
    queries = qt_ref.shape[1]
    keys = k_ref.shape[0]
    row_head = lax.broadcasted_iota(jnp.int32, (width, queries), 0) // HEAD

    def of_head(head):
        q = qt_ref[...]
        return jnp.where(row_head == head, q, jnp.zeros_like(q))

    def score(q_head, slot, c, top):
        s = dot(k_ref[c * chunk : (c + 1) * chunk, :], q_head)
        s_ref[slot, c * chunk : (c + 1) * chunk, :] = s
        return jnp.maximum(top, jnp.max(s.reshape(chunk // 8, 8, queries), axis=0))

    def low():
        return jnp.full((8, queries), -jnp.inf, f32)

    def step(head, slot, peak, more):
        if before is None:
            mixed = jnp.zeros((2 * HEAD, queries), f32)
        else:
            earlier, mixed = before(head)
            peak = jnp.maximum(peak, earlier)
            mixed = mixed * jnp.exp(earlier - peak)
        top = low()
        q_next = of_head(head + 1) if more else None
        for c in range(keys // chunk):
            if more:
                top = score(q_next, 1 - slot, c, top)
            p = jnp.exp(s_ref[slot, c * chunk : (c + 1) * chunk, :] - peak).astype(bf16)
            mixed = mixed + dot(vt_ref[head, :, c * chunk : (c + 1) * chunk], p)
        finish(head, peak, mixed)
        return jnp.max(top, axis=0, keepdims=True)

    top = low()
    q_first = of_head(0)
    for c in range(keys // chunk):
        top = score(q_first, 0, c, top)
    peak = jnp.max(top, axis=0, keepdims=True)

    def pair(i, peak):
        peak = step(2 * i, 0, peak, True)
        return step(2 * i + 1, 1, peak, True)

    peak = lax.fori_loop(0, heads // 2 - 1, pair, peak)
    peak = step(heads - 2, 0, peak, True)
    step(heads - 1, 1, peak, False)


def divide(at_ref):
    def finish(head, peak, mixed):
        at_ref[head] = (mixed[:HEAD] / mixed[HEAD:]).astype(bf16)

    return finish


def joined(at_ref):
    heads, size, queries = at_ref.shape
    return jnp.transpose(at_ref[...].reshape(heads * size, queries))


def attend_scratch(heads, queries, keys):
    width = heads * HEAD
    return [
        pltpu.VMEM((keys, width), bf16),
        pltpu.VMEM((heads, 2 * HEAD, keys), bf16),
        pltpu.VMEM((2, keys, queries), f32),
    ]


def load_values(vt_ref, values, heads):
    keys = values.shape[1]
    vt_ref[:, :HEAD, :] = values.reshape(heads, HEAD, keys)
    vt_ref[:, HEAD:, :] = jnp.ones((heads, HEAD, keys), bf16)


SCALE = 1.0 / math.sqrt(HEAD)


def across(weights, rows):
    return lax.dot_general(weights, rows, (((0,), (1,)), ((), ())), preferred_element_type=f32)


def own_kernel(
    own_ref, qkv_ref, gain_ref, qt_ref, peak_ref, mixed_ref, gain_out_ref, k, vt, s
):
    own = own_ref[...]
    gain_out_ref[...] = gain_ref[...]
    qt_ref[...] = across(qkv_ref[0], own).astype(bf16) * bf16(SCALE)
    k[...] = dot(own, qkv_ref[1]).astype(bf16)
    load_values(vt, across(qkv_ref[2], own).astype(bf16), H4)

    def finish(head, peak, mixed):
        peak_ref[head] = peak
        mixed_ref[head] = mixed

    attend(H4, k, qt_ref, vt, s, finish)


def other_kernel(
    other_ref,
    qkv_ref,
    qt_ref,
    peak_ref,
    mixed_ref,
    rows_ref,
    proj_ref,
    weight_ref,
    child_ref,
    place_ref,
    ends_ref,
    out_ref,
    parts_ref,
    k,
    vt,
    s,
    at,
    fine_ref,
    sems,
):
    other = other_ref[...]
    k[...] = dot(other, qkv_ref[1]).astype(bf16)
    load_values(vt, across(qkv_ref[2], other).astype(bf16), H4)
    attend(H4, k, qt_ref, vt, s, divide(at), lambda head: (peak_ref[head], mixed_ref[head]))
    fine = (rows_ref[...].astype(f32) + dot(joined(at), proj_ref[...])).astype(bf16)
    fine_ref[...] = fine
    copies = fetch([(fine_ref, out_ref)], sems)
    pool_own(fine, weight_ref, child_ref, place_ref, ends_ref, parts_ref)
    copies[0].wait()


def coarse_kernel(q_ref, both_ref, proj_ref, out_ref, k, vt, s, qt, at):
    n, width = q_ref.shape
    qt[...] = jnp.transpose(q_ref[...] * bf16(SCALE))
    k[...] = both_ref[:, :width]
    values = both_ref[:, width:]
    load_values(vt, jnp.transpose(values), width // HEAD)
    attend(width // HEAD, k, qt, vt, s, divide(at))
    terms = dot(joined(at), proj_ref[...]).astype(bf16)
    parts = out_ref.shape[0]
    for g in range(parts):
        out_ref[g] = terms[:, g * width : (g + 1) * width]


EDGE = 16


def gelu(values):
    return jax.nn.gelu(values, approximate=True).astype(bf16)


def three_terms(value):
    first = value.astype(bf16).astype(f32)
    second = (value - first).astype(bf16).astype(f32)
    return [first, second, value - first - second]


def run_starts(child_ref, n):
    nx = lax.axis_size("x")
    return child_ref[0:1, :] - lax.axis_index(PTS) * (nx * n)


def own_starts(child_ref, n):
    return run_starts(child_ref, n) - lax.axis_index("x") * n


def ahead(block, k, fill):
    return jnp.concatenate([block[k:], jnp.full((k, block.shape[1]), fill, f32)], axis=0)


def pool_own(fine, weight_ref, child_ref, place_ref, ends_ref, parts_ref):
    n = fine.shape[0]
    groups, total, width = parts_ref.shape
    room = total - EDGE
    start_row = own_starts(child_ref, n)
    last = jnp.max(
        jnp.where(start_row < n, start_row.astype(f32), -1.0), axis=1, keepdims=True
    ).astype(jnp.int32)
    tail = KIDS
    leaving = lax.broadcasted_iota(jnp.int32, (tail, width), 0) + (n - tail) >= last
    edge_row = lax.broadcasted_iota(jnp.int32, (EDGE, width), 0)
    ends = [ends_ref[i] > 0.0 for i in range(ends_ref.shape[0])]
    for g in range(groups):
        best = dot(fine, weight_ref[:, g * width : (g + 1) * width])
        lifted_tail = best[n - tail :]
        for i, end in enumerate(ends):
            best = jnp.where(end, best, jnp.maximum(best, ahead(best, 1 << i, 0.0)))
        parts_ref[g, :room, :] = dot(place_ref[...], gelu(best)).astype(bf16)
        head = jnp.max(jnp.where(leaving, lifted_tail, -jnp.inf), axis=0, keepdims=True)
        edge = jnp.zeros((EDGE, width), f32)
        for at, value in ((0, head), (8, best[0:1])):
            for i, term in enumerate(three_terms(value)):
                edge = jnp.where(edge_row == at + i, term, edge)
        parts_ref[g, room:, :] = edge.astype(bf16)


def count(hits):
    return jnp.sum(jnp.where(hits, 1.0, 0.0), axis=1, keepdims=True).astype(jnp.int32)


def pool_kernel(parts_ref, child_ref, want_ref, out_ref):
    groups, total, width = parts_ref.shape
    room = total - EDGE
    n = out_ref.shape[0]
    start_row = run_starts(child_ref, n)
    spot = lax.broadcasted_iota(jnp.int32, (room, width), 0)

    def edge(g, at):
        block = parts_ref[g, room:, :].astype(f32)
        return block[at : at + 1] + block[at + 1 : at + 2] + block[at + 2 : at + 3]

    parts = []
    for g in range(groups):
        part = parts_ref[g, :room, :]
        if g + 1 < groups:
            whole = gelu(jnp.maximum(edge(g, 0), edge(g + 1, 8))).astype(f32)
            final = count(start_row < (g + 1) * n) - count(start_row < g * n) - 1
            final = jnp.where(count(start_row == (g + 1) * n) > 0, -1, final)
            part = jnp.where(spot == final, whole, part.astype(f32)).astype(bf16)
        parts.append(part)
    out_ref[...] = dot(want_ref[...], jnp.concatenate(parts, axis=0)).astype(bf16)


def spread_kernel(rows_ref, out_ref):
    nz, per_z, width = rows_ref.shape
    parts, copies, part, _ = out_ref.shape
    n = nz * per_z
    rank = per_z // parts
    at = lax.broadcasted_iota(jnp.int32, (n, 1), 0)
    pts = at // part
    source = at % part // rank * per_z + (pts % 2 * (parts // 2) + pts // 2) * rank + at % rank
    moved = dot(one_hot(source, n), rows_ref[...].reshape(n, width)).astype(bf16)
    for i in range(parts):
        for x in range(copies):
            out_ref[i, x] = moved[i * part : (i + 1) * part]


def norm5_kernel(pick_ref, parts_ref, gain_ref, qkv_ref, q_ref, kv_ref, cols_ref):
    n = pick_ref.shape[0]
    groups, width = parts_ref.shape[1], parts_ref.shape[3]
    parts = [parts_ref[:, g].reshape(n, width) for g in range(groups)]
    own = parts_ref[:, pl.ds(lax.axis_index("x"), 1)].reshape(n, width)
    picked = dot(pick_ref[...], jnp.concatenate(parts + [own], axis=1)).astype(bf16)
    rows = picked[:, : groups * width]
    cols_ref[...] = picked[:, groups * width :]
    normed = layer_norm(rows, gain_ref[...])
    q_ref[...] = dot(normed, qkv_ref[0]).astype(bf16)
    kv_ref[:, :width] = dot(normed, qkv_ref[1]).astype(bf16)
    kv_ref[:, width:] = dot(normed, qkv_ref[2]).astype(bf16)


def sum_kernel(cols_ref, parts_ref, out_ref):
    total = cols_ref[...].astype(f32)
    summed = parts_ref[0].astype(f32)
    for g in range(1, parts_ref.shape[0]):
        summed = summed + parts_ref[g].astype(f32)
    out_ref[...] = (total + summed).astype(bf16)


def shape(dims, dtype=bf16):
    return jax.ShapeDtypeStruct(dims, dtype)


def exchange(block, axes):
    return lax.all_to_all(block, axes, split_axis=0, concat_axis=0, tiled=True)


VMEM = pl.BlockSpec(memory_space=pltpu.VMEM)
HBM = pl.BlockSpec(memory_space=pltpu.HBM)
DMA = pltpu.SemaphoreType.DMA


def kernel(body, name, out_shape, scratch=(), flops=0, **extra):
    extra["cost_estimate"] = pl.CostEstimate(
        flops=flops or 1 << 28, bytes_accessed=0, transcendentals=0
    )
    return pl.pallas_call(
        body,
        out_shape=out_shape,
        scratch_shapes=list(scratch),
        compiler_params=pltpu.CompilerParams(vmem_limit_bytes=48 << 20),
        name=name,
        **extra,
    )


def local(
    feats4, order4, gain4, qkv4, proj4, pool_weight, child5, mask5, order5, gain5, qkv5, proj5
):
    n = feats4.shape[0]
    nz = lax.axis_size("z")
    planes = lax.axis_size("y") * lax.axis_size("c") * lax.axis_size("x")
    nx = lax.axis_size("x")

    feats4_pair = lax.all_gather(feats4, "c", axis=0, tiled=True)
    wanted, owner4, slot5 = kernel(
        functools.partial(request_kernel, planes),
        "request",
        [shape((nz, 4, planes // 2), jnp.int32), shape((1, n), jnp.int32), shape((1, n), jnp.int32)],
    )(jnp.stack([order4, order5]))
    by_z = exchange(wanted, ("z",)).transpose(2, 1, 0)
    asked = exchange(by_z.reshape(planes // 2, 4 * nz), ("y", "x"))
    asked_both = lax.all_gather(asked, "c", axis=0, tiled=True)

    chips = n // 2
    outgoing = kernel(pick_kernel, "pick4", shape((chips, 2 * C4)))(asked, feats4_pair)
    arrived = exchange(outgoing.reshape(chips, 4, C4 // 2), CHIPS).reshape(chips, 2 * C4)
    child_rows = child5.T
    width = C5 // nx
    square = shape((n, n))
    room = n - (nx - 1) * (n // KIDS)
    room += -room % EDGE + EDGE
    pick4, pick5, want5, place, ends, gain4 = kernel(
        prepare_kernel,
        "prepare",
        [
            square,
            square,
            shape((n, nx * room)),
            shape((room, n)),
            shape((3, n, width), f32),
            shape((1, C4), f32),
        ],
    )(owner4, slot5, asked_both, child_rows, gain4.reshape(1, C4))
    curve_rows, normed4 = kernel(norm4_kernel, "norm4", [shape((n, C4)), shape((n, C4))])(
        pick4, arrived, gain4
    )
    other4 = lax.ppermute(normed4, "x", [(i, i ^ 1) for i in range(nx)])
    half = 4 * n * n * C4 * H4
    qt4, peak4, mixed4, gain5 = kernel(
        own_kernel,
        "attend4_own",
        [
            shape((C4, n)),
            shape((H4, 1, n), f32),
            shape((H4, 2 * HEAD, n), f32),
            shape((1, C5), f32),
        ],
        attend_scratch(H4, n, n),
        flops=half,
    )(normed4, qkv4, gain5.reshape(1, C5))
    fine_out, parts4 = kernel(
        other_kernel,
        "attend4_other",
        [shape((n, C4)), shape((nx, room + EDGE, width))],
        attend_scratch(H4, n, n)
        + [pltpu.VMEM((H4, HEAD, n), bf16), pltpu.VMEM((n, C4), bf16), DMA((1,))],
        flops=half,
        out_specs=[pl.BlockSpec(memory_space=pl.ANY), VMEM],
    )(other4, qkv4, qt4, peak4, mixed4, curve_rows, proj4, pool_weight, child_rows, place, ends)

    pooled = kernel(pool_kernel, "pool", shape((n, width)))(
        exchange(parts4, "x"), child_rows, want5
    )
    by_z = exchange(pooled.reshape(nz, n // nz, width), ("z",))
    copies = kernel(
        spread_kernel, "spread", shape((planes // nx, nx, n * nx // planes, width))
    )(by_z)
    parts5 = exchange(copies.reshape(planes, n * nx // planes, width), PLANE)
    parts5 = parts5.reshape(copies.shape)
    query5, kv5, own_columns = kernel(
        norm5_kernel,
        "norm5",
        [shape((n, width)), shape((n, 2 * width)), shape((n, width))],
    )(pick5, parts5, gain5, qkv5)
    both5 = lax.all_gather(kv5, "c", axis=0, tiled=True)
    terms = kernel(
        coarse_kernel,
        "attend5",
        shape((nx, n, width)),
        attend_scratch(width // HEAD, n, 2 * n)
        + [pltpu.VMEM((width, n), bf16), pltpu.VMEM((width // HEAD, HEAD, n), bf16)],
    )(query5, both5, proj5)
    coarse_out = kernel(sum_kernel, "add5", shape((n, width)))(own_columns, exchange(terms, "x"))
    return (fine_out, coarse_out)


def solution(mesh):
    pts, grp = mesh.devices.shape
    inner = Mesh(mesh.devices.reshape(pts // 8, 4, 2, grp), ALL)
    in_specs = (
        P(ALL, None),
        P(ALL),
        P(),
        P(),
        P(),
        P(),
        P(PTS, None),
        P(PTS, None),
        P(PTS),
        P(),
        P(None, None, "x"),
        P("x", None),
    )
    out_specs = (P(ALL, None), P(PTS, "x"))
    return jax.shard_map(local, mesh=inner, in_specs=in_specs, out_specs=out_specs, check_vma=False)
```

```python
import functools
import math

import jax
import jax.numpy as jnp
from jax import lax
from jax.experimental import pallas as pl
from jax.experimental.pallas import tpu as pltpu
from jax.sharding import Mesh
from jax.sharding import PartitionSpec as P

C4 = 256
H4 = 16
C5 = 512
H5 = 32
HEAD = 16
KIDS = 8

epsilon = 1e-05
f32 = jnp.float32
bf16 = jnp.bfloat16

PTS = ("z", "y", "c")
PLANE = ("y", "c", "x")
CHIPS = ("z", "y", "x")
ALL = ("z", "y", "c", "x")


def dot(a, b):
    return jnp.dot(a, b, preferred_element_type=f32)


def column(row):
    return jnp.transpose(jnp.broadcast_to(row, (8, row.shape[1])))[:, :1]


def one_hot(col, width):
    lanes = lax.broadcasted_iota(jnp.int32, (col.shape[0], width), 1)
    return jnp.where(col == lanes, 1.0, 0.0).astype(bf16)


def layer_norm(rows_in, norm_gain):
    values = rows_in.astype(f32)
    center = values - jnp.mean(values, axis=-1, keepdims=True)
    spread = jnp.mean(center * center, axis=-1, keepdims=True)
    return (center * lax.rsqrt(spread + epsilon) * norm_gain).astype(bf16)


def fetch(pairs, sems):
    copies = [pltpu.make_async_copy(a, b, sems.at[i]) for i, (a, b) in enumerate(pairs)]
    for copy in copies:
        copy.start()
    return copies


def request_kernel(planes, orders_ref, out_ref, owner_ref, slot_ref):
    o4, o5 = orders_ref[0:1, :], orders_ref[1:2, :]
    n = o4.shape[1]
    nz, nx = out_ref.shape[0], lax.axis_size("x")
    x = lax.axis_index("x")
    owner4, owner5 = o4 // n, o5 // n
    ny, half, per_z = planes // (2 * nx), planes // 2, planes // nx
    u = owner4 % planes
    lane4 = u // nx % 2 * half + u // (2 * nx) * nx + u % nx
    owner_ref[...] = u // nx % 2 * (n // 2) + owner4 // planes * half + lane4 % half
    of_pts = owner5 % per_z
    pair5 = of_pts % 2 * ny + of_pts // 2

    lanes = lax.broadcasted_iota(jnp.int32, (n, n), 1)
    rows = lax.broadcasted_iota(jnp.int32, (n, n), 0)
    earlier = jnp.where((column(owner5) == owner5) & (rows < lanes), 1.0, 0.0)
    rank = jnp.sum(earlier, axis=0, keepdims=True).astype(jnp.int32)
    slot_ref[...] = (of_pts * nz + owner5 // per_z) * nx + rank

    place = lax.broadcasted_iota(jnp.int32, (planes, n), 0)
    zs = lax.broadcasted_iota(jnp.int32, (nz, n), 0)

    def table(z_hit, u_hit, row):
        low = jnp.where(u_hit, (row % 256).astype(f32), 0.0)
        high = jnp.where(u_hit, (row // 256).astype(f32), 0.0)
        both = lax.dot_general(
            jnp.where(z_hit, 1.0, 0.0).astype(bf16),
            jnp.concatenate([low, high], axis=0).astype(bf16),
            (((1,), (1,)), ((), ())),
            preferred_element_type=f32,
        )
        return (both[:, :planes] + 256.0 * both[:, planes:]).astype(jnp.int32)

    want4 = table(zs == owner4 // planes, place == lane4, o4 % n)
    own_rank = (zs == owner5 // per_z) & (rank == x)
    want5 = table(own_rank, place // nx == pair5, o5 % n)
    for c in range(2):
        out_ref[:, c, :] = want4[:, c * half : (c + 1) * half]
        out_ref[:, 2 + c, :] = want5[:, c * half : (c + 1) * half]


def picks(cols, width):
    return jnp.concatenate([one_hot(cols[:, i : i + 1], width) for i in range(cols.shape[1])], axis=0)


def pick_kernel(asked_ref, table_ref, out_ref):
    nz = asked_ref.shape[1] // 4
    n, width = table_ref.shape[0] // 2, table_ref.shape[1]
    for c in range(2):
        pick = picks(asked_ref[:, c * nz : (c + 1) * nz], n)
        out_ref[:, c * width : (c + 1) * width] = dot(
            pick, table_ref[c * n : (c + 1) * n, :]
        ).astype(bf16)


def prepare_kernel(
    owner_ref,
    slot_ref,
    asked_ref,
    child_ref,
    gain_ref,
    pick4_ref,
    pick5_ref,
    want5_ref,
    place_ref,
    ends_ref,
    gain_out_ref,
):
    gain_out_ref[...] = gain_ref[...]
    n = owner_ref.shape[1]
    points = child_ref.shape[1]
    pick4_ref[...] = one_hot(column(owner_ref[...]), n)
    pick5_ref[...] = one_hot(column(slot_ref[...]), n)

    start_row = run_starts(child_ref, n)
    room = place_ref.shape[0]
    at = lax.broadcasted_iota(jnp.int32, (1, points), 1)
    for g in range(want5_ref.shape[1] // room):
        before = count(start_row < g * n)
        at = jnp.where(start_row // n == g, at - before + g * room, at)
    nz = asked_ref.shape[1] // 4
    asked5 = jnp.where(
        lax.axis_index("c") == 0, asked_ref[:, 2 * nz : 3 * nz], asked_ref[:, 3 * nz :]
    )
    wanted = picks(asked5, points).astype(f32)
    spot = jnp.sum(wanted * at.astype(f32), axis=1, keepdims=True).astype(jnp.int32)
    want5_ref[...] = one_hot(spot, want5_ref.shape[1])

    own_row = own_starts(child_ref, n)
    own = column(own_row)
    lanes = lax.broadcasted_iota(jnp.int32, (points, n), 1)
    opened = jnp.where((own >= 0) & (own <= lanes), 1.0, 0.0)
    number = jnp.sum(opened, axis=0, keepdims=True).astype(jnp.int32) - 1
    opens_here = jnp.sum(jnp.where(own == lanes, 1.0, 0.0), axis=0, keepdims=True)
    spots = lax.broadcasted_iota(jnp.int32, (room, n), 0)
    place_ref[...] = jnp.where((spots == number) & (opens_here > 0.0), 1.0, 0.0).astype(bf16)

    rows = lax.broadcasted_iota(jnp.int32, (n, points), 0)
    first = jnp.where(own_row == rows, 1.0, 0.0).astype(bf16)
    opens = dot(first, jnp.ones((points, ends_ref.shape[2]), bf16))
    cut = ahead(opens, 1, 1.0)
    for i in range(ends_ref.shape[0]):
        ends_ref[i] = cut
        cut = jnp.maximum(cut, ahead(cut, 1 << i, 1.0))


def norm4_kernel(pick_ref, arrived_ref, gain_ref, rows_ref, normed_ref):
    width = rows_ref.shape[1]
    arrived = jnp.concatenate([arrived_ref[:, :width], arrived_ref[:, width:]], axis=0)
    rows = dot(pick_ref[...], arrived).astype(bf16)
    rows_ref[...] = rows
    normed_ref[...] = layer_norm(rows, gain_ref[...])


def attend(heads, k_ref, qt_ref, vt_ref, s_ref, finish, before=None, chunk=512):
    width = heads * HEAD
    queries = qt_ref.shape[1]
    keys = k_ref.shape[0]
    row_head = lax.broadcasted_iota(jnp.int32, (width, queries), 0) // HEAD

    def of_head(head):
        q = qt_ref[...]
        return jnp.where(row_head == head, q, jnp.zeros_like(q))

    def score(q_head, slot, c, top):
        s = dot(k_ref[c * chunk : (c + 1) * chunk, :], q_head)
        s_ref[slot, c * chunk : (c + 1) * chunk, :] = s
        return jnp.maximum(top, jnp.max(s.reshape(chunk // 8, 8, queries), axis=0))

    def low():
        return jnp.full((8, queries), -jnp.inf, f32)

    def step(head, slot, peak, more):
        if before is None:
            mixed = jnp.zeros((2 * HEAD, queries), f32)
        else:
            earlier, mixed = before(head)
            peak = jnp.maximum(peak, earlier)
            mixed = mixed * jnp.exp(earlier - peak)
        top = low()
        q_next = of_head(head + 1) if more else None
        for c in range(keys // chunk):
            if more:
                top = score(q_next, 1 - slot, c, top)
            p = jnp.exp(s_ref[slot, c * chunk : (c + 1) * chunk, :] - peak).astype(bf16)
            mixed = mixed + dot(vt_ref[head, :, c * chunk : (c + 1) * chunk], p)
        finish(head, peak, mixed)
        return jnp.max(top, axis=0, keepdims=True)

    top = low()
    q_first = of_head(0)
    for c in range(keys // chunk):
        top = score(q_first, 0, c, top)
    peak = jnp.max(top, axis=0, keepdims=True)

    def pair(i, peak):
        peak = step(2 * i, 0, peak, True)
        return step(2 * i + 1, 1, peak, True)

    peak = lax.fori_loop(0, heads // 2 - 1, pair, peak)
    peak = step(heads - 2, 0, peak, True)
    step(heads - 1, 1, peak, False)


def divide(at_ref):
    def finish(head, peak, mixed):
        at_ref[head] = (mixed[:HEAD] / mixed[HEAD:]).astype(bf16)

    return finish


def joined(at_ref):
    heads, size, queries = at_ref.shape
    return jnp.transpose(at_ref[...].reshape(heads * size, queries))


def attend_scratch(heads, queries, keys):
    width = heads * HEAD
    return [
        pltpu.VMEM((keys, width), bf16),
        pltpu.VMEM((heads, 2 * HEAD, keys), bf16),
        pltpu.VMEM((2, keys, queries), f32),
    ]


def load_values(vt_ref, values, heads):
    keys = values.shape[1]
    vt_ref[:, :HEAD, :] = values.reshape(heads, HEAD, keys)
    vt_ref[:, HEAD:, :] = jnp.ones((heads, HEAD, keys), bf16)


SCALE = 1.0 / math.sqrt(HEAD)


def across(weights, rows):
    return lax.dot_general(weights, rows, (((0,), (1,)), ((), ())), preferred_element_type=f32)


def own_kernel(
    own_ref, qkv_ref, gain_ref, qt_ref, peak_ref, mixed_ref, gain_out_ref, k, vt, s
):
    own = own_ref[...]
    gain_out_ref[...] = gain_ref[...]
    qt_ref[...] = across(qkv_ref[0], own).astype(bf16) * bf16(SCALE)
    k[...] = dot(own, qkv_ref[1]).astype(bf16)
    load_values(vt, across(qkv_ref[2], own).astype(bf16), H4)

    def finish(head, peak, mixed):
        peak_ref[head] = peak
        mixed_ref[head] = mixed

    attend(H4, k, qt_ref, vt, s, finish)


def other_kernel(
    other_ref,
    qkv_ref,
    qt_ref,
    peak_ref,
    mixed_ref,
    rows_ref,
    proj_ref,
    weight_ref,
    child_ref,
    place_ref,
    ends_ref,
    out_ref,
    parts_ref,
    k,
    vt,
    s,
    at,
    fine_ref,
    sems,
):
    other = other_ref[...]
    k[...] = dot(other, qkv_ref[1]).astype(bf16)
    load_values(vt, across(qkv_ref[2], other).astype(bf16), H4)
    attend(H4, k, qt_ref, vt, s, divide(at), lambda head: (peak_ref[head], mixed_ref[head]))
    fine = (rows_ref[...].astype(f32) + dot(joined(at), proj_ref[...])).astype(bf16)
    fine_ref[...] = fine
    copies = fetch([(fine_ref, out_ref)], sems)
    pool_own(fine, weight_ref, child_ref, place_ref, ends_ref, parts_ref)
    copies[0].wait()


def coarse_kernel(q_ref, both_ref, proj_ref, out_ref, k, vt, s, qt, at):
    n, width = q_ref.shape
    qt[...] = jnp.transpose(q_ref[...] * bf16(SCALE))
    k[...] = both_ref[:, :width]
    values = both_ref[:, width:]
    load_values(vt, jnp.transpose(values), width // HEAD)
    attend(width // HEAD, k, qt, vt, s, divide(at))
    terms = dot(joined(at), proj_ref[...]).astype(bf16)
    parts = out_ref.shape[0]
    for g in range(parts):
        out_ref[g] = terms[:, g * width : (g + 1) * width]


EDGE = 16


def gelu(values):
    return jax.nn.gelu(values, approximate=True).astype(bf16)


def three_terms(value):
    first = value.astype(bf16).astype(f32)
    second = (value - first).astype(bf16).astype(f32)
    return [first, second, value - first - second]


def run_starts(child_ref, n):
    nx = lax.axis_size("x")
    return child_ref[0:1, :] - lax.axis_index(PTS) * (nx * n)


def own_starts(child_ref, n):
    return run_starts(child_ref, n) - lax.axis_index("x") * n


def ahead(block, k, fill):
    return jnp.concatenate([block[k:], jnp.full((k, block.shape[1]), fill, f32)], axis=0)


def pool_own(fine, weight_ref, child_ref, place_ref, ends_ref, parts_ref):
    n = fine.shape[0]
    groups, total, width = parts_ref.shape
    room = total - EDGE
    start_row = own_starts(child_ref, n)
    last = jnp.max(
        jnp.where(start_row < n, start_row.astype(f32), -1.0), axis=1, keepdims=True
    ).astype(jnp.int32)
    tail = KIDS
    leaving = lax.broadcasted_iota(jnp.int32, (tail, width), 0) + (n - tail) >= last
    edge_row = lax.broadcasted_iota(jnp.int32, (EDGE, width), 0)
    ends = [ends_ref[i] > 0.0 for i in range(ends_ref.shape[0])]
    for g in range(groups):
        best = dot(fine, weight_ref[:, g * width : (g + 1) * width])
        lifted_tail = best[n - tail :]
        for i, end in enumerate(ends):
            best = jnp.where(end, best, jnp.maximum(best, ahead(best, 1 << i, 0.0)))
        parts_ref[g, :room, :] = dot(place_ref[...], gelu(best)).astype(bf16)
        head = jnp.max(jnp.where(leaving, lifted_tail, -jnp.inf), axis=0, keepdims=True)
        edge = jnp.zeros((EDGE, width), f32)
        for at, value in ((0, head), (8, best[0:1])):
            for i, term in enumerate(three_terms(value)):
                edge = jnp.where(edge_row == at + i, term, edge)
        parts_ref[g, room:, :] = edge.astype(bf16)


def count(hits):
    return jnp.sum(jnp.where(hits, 1.0, 0.0), axis=1, keepdims=True).astype(jnp.int32)


def pool_kernel(parts_ref, child_ref, want_ref, out_ref):
    groups, total, width = parts_ref.shape
    room = total - EDGE
    n = out_ref.shape[0]
    start_row = run_starts(child_ref, n)
    spot = lax.broadcasted_iota(jnp.int32, (room, width), 0)

    def edge(g, at):
        block = parts_ref[g, room:, :].astype(f32)
        return block[at : at + 1] + block[at + 1 : at + 2] + block[at + 2 : at + 3]

    parts = []
    for g in range(groups):
        part = parts_ref[g, :room, :]
        if g + 1 < groups:
            whole = gelu(jnp.maximum(edge(g, 0), edge(g + 1, 8))).astype(f32)
            final = count(start_row < (g + 1) * n) - count(start_row < g * n) - 1
            final = jnp.where(count(start_row == (g + 1) * n) > 0, -1, final)
            part = jnp.where(spot == final, whole, part.astype(f32)).astype(bf16)
        parts.append(part)
    out_ref[...] = dot(want_ref[...], jnp.concatenate(parts, axis=0)).astype(bf16)


def spread_kernel(rows_ref, out_ref):
    nz, per_z, width = rows_ref.shape
    parts, copies, part, _ = out_ref.shape
    n = nz * per_z
    rank = per_z // parts
    at = lax.broadcasted_iota(jnp.int32, (n, 1), 0)
    pts = at // part
    source = at % part // rank * per_z + (pts % 2 * (parts // 2) + pts // 2) * rank + at % rank
    moved = dot(one_hot(source, n), rows_ref[...].reshape(n, width)).astype(bf16)
    for i in range(parts):
        for x in range(copies):
            out_ref[i, x] = moved[i * part : (i + 1) * part]


def norm5_kernel(pick_ref, parts_ref, gain_ref, qkv_ref, q_ref, kv_ref, cols_ref):
    n = pick_ref.shape[0]
    groups, width = parts_ref.shape[1], parts_ref.shape[3]
    parts = [parts_ref[:, g].reshape(n, width) for g in range(groups)]
    own = parts_ref[:, pl.ds(lax.axis_index("x"), 1)].reshape(n, width)
    picked = dot(pick_ref[...], jnp.concatenate(parts + [own], axis=1)).astype(bf16)
    rows = picked[:, : groups * width]
    cols_ref[...] = picked[:, groups * width :]
    normed = layer_norm(rows, gain_ref[...])
    weights = jnp.concatenate([qkv_ref[i] for i in range(3)], axis=1)
    projected = dot(normed, weights).astype(bf16)
    q_ref[...] = projected[:, :width]
    kv_ref[...] = projected[:, width:]


def sum_kernel(cols_ref, parts_ref, out_ref):
    total = cols_ref[...].astype(f32)
    summed = parts_ref[0].astype(f32)
    for g in range(1, parts_ref.shape[0]):
        summed = summed + parts_ref[g].astype(f32)
    out_ref[...] = (total + summed).astype(bf16)


def shape(dims, dtype=bf16):
    return jax.ShapeDtypeStruct(dims, dtype)


def exchange(block, axes):
    return lax.all_to_all(block, axes, split_axis=0, concat_axis=0, tiled=True)


VMEM = pl.BlockSpec(memory_space=pltpu.VMEM)
HBM = pl.BlockSpec(memory_space=pltpu.HBM)
DMA = pltpu.SemaphoreType.DMA


def kernel(body, name, out_shape, scratch=(), flops=0, **extra):
    extra["cost_estimate"] = pl.CostEstimate(
        flops=flops or 1 << 28, bytes_accessed=0, transcendentals=0
    )
    return pl.pallas_call(
        body,
        out_shape=out_shape,
        scratch_shapes=list(scratch),
        compiler_params=pltpu.CompilerParams(vmem_limit_bytes=48 << 20),
        name=name,
        **extra,
    )


def local(
    feats4, order4, gain4, qkv4, proj4, pool_weight, child5, mask5, order5, gain5, qkv5, proj5
):
    n = feats4.shape[0]
    nz = lax.axis_size("z")
    planes = lax.axis_size("y") * lax.axis_size("c") * lax.axis_size("x")
    nx = lax.axis_size("x")

    feats4_pair = lax.all_gather(feats4, "c", axis=0, tiled=True)
    wanted, owner4, slot5 = kernel(
        functools.partial(request_kernel, planes),
        "request",
        [shape((nz, 4, planes // 2), jnp.int32), shape((1, n), jnp.int32), shape((1, n), jnp.int32)],
    )(jnp.stack([order4, order5]))
    by_z = exchange(wanted, ("z",)).transpose(2, 1, 0)
    by_z, feats4_pair = lax.optimization_barrier((by_z, feats4_pair))
    asked = exchange(by_z.reshape(planes // 2, 4 * nz), ("y", "x"))
    asked_both = lax.all_gather(asked, "c", axis=0, tiled=True)

    chips = n // 2
    outgoing = kernel(pick_kernel, "pick4", shape((chips, 2 * C4)))(asked, feats4_pair)
    arrived = exchange(outgoing.reshape(chips, 4, C4 // 2), CHIPS).reshape(chips, 2 * C4)
    child_rows = child5.T
    width = C5 // nx
    square = shape((n, n))
    room = n - (nx - 1) * (n // KIDS)
    room += -room % EDGE + EDGE
    pick4, pick5, want5, place, ends, gain4 = kernel(
        prepare_kernel,
        "prepare",
        [
            square,
            square,
            shape((n, nx * room)),
            shape((room, n)),
            shape((3, n, width), f32),
            shape((1, C4), f32),
        ],
    )(owner4, slot5, asked_both, child_rows, gain4.reshape(1, C4))
    curve_rows, normed4 = kernel(norm4_kernel, "norm4", [shape((n, C4)), shape((n, C4))])(
        pick4, arrived, gain4
    )
    other4 = lax.ppermute(normed4, "x", [(i, i ^ 1) for i in range(nx)])
    half = 4 * n * n * C4 * H4
    qt4, peak4, mixed4, gain5 = kernel(
        own_kernel,
        "attend4_own",
        [
            shape((C4, n)),
            shape((H4, 1, n), f32),
            shape((H4, 2 * HEAD, n), f32),
            shape((1, C5), f32),
        ],
        attend_scratch(H4, n, n),
        flops=half,
    )(normed4, qkv4, gain5.reshape(1, C5))
    fine_out, parts4 = kernel(
        other_kernel,
        "attend4_other",
        [shape((n, C4)), shape((nx, room + EDGE, width))],
        attend_scratch(H4, n, n)
        + [pltpu.VMEM((H4, HEAD, n), bf16), pltpu.VMEM((n, C4), bf16), DMA((1,))],
        flops=half,
        out_specs=[pl.BlockSpec(memory_space=pl.ANY), VMEM],
    )(other4, qkv4, qt4, peak4, mixed4, curve_rows, proj4, pool_weight, child_rows, place, ends)

    pooled = kernel(pool_kernel, "pool", shape((n, width)))(
        exchange(parts4, "x"), child_rows, want5
    )
    by_z = exchange(pooled.reshape(nz, n // nz, width), ("z",))
    copies = kernel(
        spread_kernel, "spread", shape((planes // nx, nx, n * nx // planes, width))
    )(by_z)
    parts5 = exchange(copies.reshape(planes, n * nx // planes, width), PLANE)
    parts5 = parts5.reshape(copies.shape)
    query5, kv5, own_columns = kernel(
        norm5_kernel,
        "norm5",
        [shape((n, width)), shape((n, 2 * width)), shape((n, width))],
    )(pick5, parts5, gain5, qkv5)
    both5 = lax.all_gather(kv5, "c", axis=0, tiled=True)
    terms = kernel(
        coarse_kernel,
        "attend5",
        shape((nx, n, width)),
        attend_scratch(width // HEAD, n, 2 * n)
        + [pltpu.VMEM((width, n), bf16), pltpu.VMEM((width // HEAD, HEAD, n), bf16)],
    )(query5, both5, proj5)
    coarse_out = kernel(sum_kernel, "add5", shape((n, width)))(own_columns, exchange(terms, "x"))
    return (fine_out, coarse_out)


def solution(mesh):
    pts, grp = mesh.devices.shape
    inner = Mesh(mesh.devices.reshape(pts // 8, 4, 2, grp), ALL)
    in_specs = (
        P(ALL, None),
        P(ALL),
        P(),
        P(),
        P(),
        P(),
        P(PTS, None),
        P(PTS, None),
        P(PTS),
        P(),
        P(None, None, "x"),
        P("x", None),
    )
    out_specs = (P(ALL, None), P(PTS, "x"))
    return jax.shard_map(local, mesh=inner, in_specs=in_specs, out_specs=out_specs, check_vma=False)
```

```python
import functools
import math

import jax
import jax.numpy as jnp
from jax import lax
from jax.experimental import pallas as pl
from jax.experimental.pallas import tpu as pltpu
from jax.sharding import Mesh
from jax.sharding import PartitionSpec as P

C4 = 256
H4 = 16
C5 = 512
H5 = 32
HEAD = 16
KIDS = 8

epsilon = 1e-05
f32 = jnp.float32
bf16 = jnp.bfloat16

PTS = ("z", "y", "c")
PLANE = ("y", "c", "x")
CHIPS = ("z", "y", "x")
ALL = ("z", "y", "c", "x")


def dot(a, b):
    return jnp.dot(a, b, preferred_element_type=f32)


def column(row):
    return jnp.transpose(jnp.broadcast_to(row, (8, row.shape[1])))[:, :1]


def one_hot(col, width):
    lanes = lax.broadcasted_iota(jnp.int32, (col.shape[0], width), 1)
    return jnp.where(col == lanes, 1.0, 0.0).astype(bf16)


def layer_norm(rows_in, norm_gain):
    values = rows_in.astype(f32)
    center = values - jnp.mean(values, axis=-1, keepdims=True)
    spread = jnp.mean(center * center, axis=-1, keepdims=True)
    return (center * lax.rsqrt(spread + epsilon) * norm_gain).astype(bf16)


def fetch(pairs, sems):
    copies = [pltpu.make_async_copy(a, b, sems.at[i]) for i, (a, b) in enumerate(pairs)]
    for copy in copies:
        copy.start()
    return copies


def request_kernel(planes, orders_ref, out_ref, owner_ref, slot_ref):
    o4, o5 = orders_ref[0:1, :], orders_ref[1:2, :]
    n = o4.shape[1]
    nz, nx = out_ref.shape[0], lax.axis_size("x")
    x = lax.axis_index("x")
    owner4, owner5 = o4 // n, o5 // n
    ny, half, per_z = planes // (2 * nx), planes // 2, planes // nx
    u = owner4 % planes
    lane4 = u // nx % 2 * half + u // (2 * nx) * nx + u % nx
    owner_ref[...] = u // nx % 2 * (n // 2) + owner4 // planes * half + lane4 % half
    of_pts = owner5 % per_z
    pair5 = of_pts % 2 * ny + of_pts // 2

    lanes = lax.broadcasted_iota(jnp.int32, (n, n), 1)
    rows = lax.broadcasted_iota(jnp.int32, (n, n), 0)
    earlier = jnp.where((column(owner5) == owner5) & (rows < lanes), 1.0, 0.0)
    rank = jnp.sum(earlier, axis=0, keepdims=True).astype(jnp.int32)
    slot_ref[...] = (of_pts * nz + owner5 // per_z) * nx + rank

    place = lax.broadcasted_iota(jnp.int32, (planes, n), 0)
    zs = lax.broadcasted_iota(jnp.int32, (nz, n), 0)

    def table(z_hit, u_hit, row):
        low = jnp.where(u_hit, (row % 256).astype(f32), 0.0)
        high = jnp.where(u_hit, (row // 256).astype(f32), 0.0)
        both = lax.dot_general(
            jnp.where(z_hit, 1.0, 0.0).astype(bf16),
            jnp.concatenate([low, high], axis=0).astype(bf16),
            (((1,), (1,)), ((), ())),
            preferred_element_type=f32,
        )
        return (both[:, :planes] + 256.0 * both[:, planes:]).astype(jnp.int32)

    want4 = table(zs == owner4 // planes, place == lane4, o4 % n)
    own_rank = (zs == owner5 // per_z) & (rank == x)
    want5 = table(own_rank, place // nx == pair5, o5 % n)
    for c in range(2):
        out_ref[:, c, :] = want4[:, c * half : (c + 1) * half]
        out_ref[:, 2 + c, :] = want5[:, c * half : (c + 1) * half]


def picks(cols, width):
    return jnp.concatenate([one_hot(cols[:, i : i + 1], width) for i in range(cols.shape[1])], axis=0)


def pick_kernel(asked_ref, table_ref, out_ref):
    nz = asked_ref.shape[1] // 4
    n, width = table_ref.shape[0] // 2, table_ref.shape[1]
    for c in range(2):
        pick = picks(asked_ref[:, c * nz : (c + 1) * nz], n)
        out_ref[:, c * width : (c + 1) * width] = dot(
            pick, table_ref[c * n : (c + 1) * n, :]
        ).astype(bf16)


def prepare_kernel(
    owner_ref,
    slot_ref,
    asked_ref,
    child_ref,
    gain_ref,
    pick4_ref,
    pick5_ref,
    want5_ref,
    place_ref,
    ends_ref,
    gain_out_ref,
):
    gain_out_ref[...] = gain_ref[...]
    n = owner_ref.shape[1]
    points = child_ref.shape[1]
    pick4_ref[...] = one_hot(column(owner_ref[...]), n)
    pick5_ref[...] = one_hot(column(slot_ref[...]), n)

    start_row = run_starts(child_ref, n)
    room = place_ref.shape[0]
    at = lax.broadcasted_iota(jnp.int32, (1, points), 1)
    for g in range(want5_ref.shape[1] // room):
        before = count(start_row < g * n)
        at = jnp.where(start_row // n == g, at - before + g * room, at)
    nz = asked_ref.shape[1] // 4
    asked5 = jnp.where(
        lax.axis_index("c") == 0, asked_ref[:, 2 * nz : 3 * nz], asked_ref[:, 3 * nz :]
    )
    wanted = picks(asked5, points).astype(f32)
    spot = jnp.sum(wanted * at.astype(f32), axis=1, keepdims=True).astype(jnp.int32)
    want5_ref[...] = one_hot(spot, want5_ref.shape[1])

    own_row = own_starts(child_ref, n)
    own = column(own_row)
    lanes = lax.broadcasted_iota(jnp.int32, (points, n), 1)
    opened = jnp.where((own >= 0) & (own <= lanes), 1.0, 0.0)
    number = jnp.sum(opened, axis=0, keepdims=True).astype(jnp.int32) - 1
    opens_here = jnp.sum(jnp.where(own == lanes, 1.0, 0.0), axis=0, keepdims=True)
    spots = lax.broadcasted_iota(jnp.int32, (room, n), 0)
    place_ref[...] = jnp.where((spots == number) & (opens_here > 0.0), 1.0, 0.0).astype(bf16)

    rows = lax.broadcasted_iota(jnp.int32, (n, points), 0)
    first = jnp.where(own_row == rows, 1.0, 0.0).astype(bf16)
    opens = dot(first, jnp.ones((points, ends_ref.shape[2]), bf16))
    cut = ahead(opens, 1, 1.0)
    for i in range(ends_ref.shape[0]):
        ends_ref[i] = cut
        cut = jnp.maximum(cut, ahead(cut, 1 << i, 1.0))


def norm4_kernel(pick_ref, arrived_ref, gain_ref, rows_ref, normed_ref):
    width = rows_ref.shape[1]
    arrived = jnp.concatenate([arrived_ref[:, :width], arrived_ref[:, width:]], axis=0)
    rows = dot(pick_ref[...], arrived).astype(bf16)
    rows_ref[...] = rows
    normed_ref[...] = layer_norm(rows, gain_ref[...])


TOGETHER = 2
SUMS = (TOGETHER + 1) * HEAD


def attend(heads, k_ref, qt_ref, vt_ref, s_ref, finish, before=None, chunk=512):
    steps = heads // TOGETHER
    queries = s_ref.shape[2]
    keys = k_ref.shape[0]
    row_head = lax.broadcasted_iota(jnp.int32, qt_ref.shape, 0) // HEAD

    def of_step(step):
        q = qt_ref[...]
        none = jnp.zeros_like(q)
        each = [jnp.where(row_head == step * TOGETHER + i, q, none) for i in range(TOGETHER)]
        return jnp.concatenate(each, axis=1)

    def score(q_head, slot, c, top):
        s = dot(k_ref[c * chunk : (c + 1) * chunk, :], q_head)
        s_ref[slot, c * chunk : (c + 1) * chunk, :] = s
        return jnp.maximum(top, jnp.max(s.reshape(chunk // 8, 8, queries), axis=0))

    def low():
        return jnp.full((8, queries), -jnp.inf, f32)

    def step(head, slot, peak, more):
        if before is None:
            mixed = jnp.zeros((SUMS, queries), f32)
        else:
            earlier, mixed = before(head)
            peak = jnp.maximum(peak, earlier)
            mixed = mixed * jnp.exp(earlier - peak)
        top = low()
        q_next = of_step(head + 1) if more else None
        for c in range(keys // chunk):
            if more:
                top = score(q_next, 1 - slot, c, top)
            p = jnp.exp(s_ref[slot, c * chunk : (c + 1) * chunk, :] - peak).astype(bf16)
            mixed = mixed + dot(vt_ref[head, :, c * chunk : (c + 1) * chunk], p)
        finish(head, peak, mixed)
        return jnp.max(top, axis=0, keepdims=True)

    top = low()
    q_first = of_step(0)
    for c in range(keys // chunk):
        top = score(q_first, 0, c, top)
    peak = jnp.max(top, axis=0, keepdims=True)

    def pair(i, peak):
        peak = step(2 * i, 0, peak, True)
        return step(2 * i + 1, 1, peak, True)

    peak = lax.fori_loop(0, steps // 2 - 1, pair, peak)
    peak = step(steps - 2, 0, peak, True)
    step(steps - 1, 1, peak, False)


def divide(at_ref):
    n = at_ref.shape[2]

    def finish(step, peak, mixed):
        for i in range(TOGETHER):
            part = mixed[i * HEAD : (i + 1) * HEAD, i * n : (i + 1) * n]
            total = mixed[TOGETHER * HEAD :, i * n : (i + 1) * n]
            at_ref[step * TOGETHER + i] = (part / total).astype(bf16)

    return finish


def joined(at_ref):
    heads, size, queries = at_ref.shape
    return jnp.transpose(at_ref[...].reshape(heads * size, queries))


def attend_scratch(heads, queries, keys):
    width = heads * HEAD
    return [
        pltpu.VMEM((keys, width), bf16),
        pltpu.VMEM((heads // TOGETHER, SUMS, keys), bf16),
        pltpu.VMEM((2, keys, TOGETHER * queries), f32),
    ]


def load_values(vt_ref, values, heads):
    keys = values.shape[1]
    own = TOGETHER * HEAD
    vt_ref[:, :own, :] = values.reshape(heads // TOGETHER, own, keys)
    vt_ref[:, own:, :] = jnp.ones((heads // TOGETHER, HEAD, keys), bf16)


SCALE = 1.0 / math.sqrt(HEAD)


def across(weights, rows):
    return lax.dot_general(weights, rows, (((0,), (1,)), ((), ())), preferred_element_type=f32)


def own_kernel(
    own_ref, qkv_ref, gain_ref, qt_ref, peak_ref, mixed_ref, gain_out_ref, k, vt, s
):
    own = own_ref[...]
    gain_out_ref[...] = gain_ref[...]
    qt_ref[...] = across(qkv_ref[0], own).astype(bf16) * bf16(SCALE)
    k[...] = dot(own, qkv_ref[1]).astype(bf16)
    load_values(vt, across(qkv_ref[2], own).astype(bf16), H4)

    def finish(head, peak, mixed):
        peak_ref[head] = peak
        mixed_ref[head] = mixed

    attend(H4, k, qt_ref, vt, s, finish)


def other_kernel(
    other_ref,
    qkv_ref,
    qt_ref,
    peak_ref,
    mixed_ref,
    rows_ref,
    proj_ref,
    weight_ref,
    child_ref,
    place_ref,
    ends_ref,
    out_ref,
    parts_ref,
    k,
    vt,
    s,
    at,
    fine_ref,
    sems,
):
    other = other_ref[...]
    k[...] = dot(other, qkv_ref[1]).astype(bf16)
    load_values(vt, across(qkv_ref[2], other).astype(bf16), H4)
    attend(H4, k, qt_ref, vt, s, divide(at), lambda head: (peak_ref[head], mixed_ref[head]))
    fine = (rows_ref[...].astype(f32) + dot(joined(at), proj_ref[...])).astype(bf16)
    fine_ref[...] = fine
    copies = fetch([(fine_ref, out_ref)], sems)
    pool_own(fine, weight_ref, child_ref, place_ref, ends_ref, parts_ref)
    copies[0].wait()


def coarse_kernel(q_ref, both_ref, proj_ref, out_ref, k, vt, s, qt, at):
    n, width = q_ref.shape
    qt[...] = jnp.transpose(q_ref[...] * bf16(SCALE))
    k[...] = both_ref[:, :width]
    values = both_ref[:, width:]
    load_values(vt, jnp.transpose(values), width // HEAD)
    attend(width // HEAD, k, qt, vt, s, divide(at))
    terms = dot(joined(at), proj_ref[...]).astype(bf16)
    parts = out_ref.shape[0]
    for g in range(parts):
        out_ref[g] = terms[:, g * width : (g + 1) * width]


EDGE = 16


def gelu(values):
    return jax.nn.gelu(values, approximate=True).astype(bf16)


def three_terms(value):
    first = value.astype(bf16).astype(f32)
    second = (value - first).astype(bf16).astype(f32)
    return [first, second, value - first - second]


def run_starts(child_ref, n):
    nx = lax.axis_size("x")
    return child_ref[0:1, :] - lax.axis_index(PTS) * (nx * n)


def own_starts(child_ref, n):
    return run_starts(child_ref, n) - lax.axis_index("x") * n


def ahead(block, k, fill):
    return jnp.concatenate([block[k:], jnp.full((k, block.shape[1]), fill, f32)], axis=0)


def pool_own(fine, weight_ref, child_ref, place_ref, ends_ref, parts_ref):
    n = fine.shape[0]
    groups, total, width = parts_ref.shape
    room = total - EDGE
    start_row = own_starts(child_ref, n)
    last = jnp.max(
        jnp.where(start_row < n, start_row.astype(f32), -1.0), axis=1, keepdims=True
    ).astype(jnp.int32)
    tail = KIDS
    leaving = lax.broadcasted_iota(jnp.int32, (tail, width), 0) + (n - tail) >= last
    edge_row = lax.broadcasted_iota(jnp.int32, (EDGE, width), 0)
    ends = [ends_ref[i] > 0.0 for i in range(ends_ref.shape[0])]
    for g in range(groups):
        best = dot(fine, weight_ref[:, g * width : (g + 1) * width])
        lifted_tail = best[n - tail :]
        for i, end in enumerate(ends):
            best = jnp.where(end, best, jnp.maximum(best, ahead(best, 1 << i, 0.0)))
        parts_ref[g, :room, :] = dot(place_ref[...], gelu(best)).astype(bf16)
        head = jnp.max(jnp.where(leaving, lifted_tail, -jnp.inf), axis=0, keepdims=True)
        edge = jnp.zeros((EDGE, width), f32)
        for at, value in ((0, head), (8, best[0:1])):
            for i, term in enumerate(three_terms(value)):
                edge = jnp.where(edge_row == at + i, term, edge)
        parts_ref[g, room:, :] = edge.astype(bf16)


def count(hits):
    return jnp.sum(jnp.where(hits, 1.0, 0.0), axis=1, keepdims=True).astype(jnp.int32)


def pool_kernel(parts_ref, child_ref, want_ref, out_ref):
    groups, total, width = parts_ref.shape
    room = total - EDGE
    n = out_ref.shape[0]
    start_row = run_starts(child_ref, n)
    spot = lax.broadcasted_iota(jnp.int32, (room, width), 0)

    def edge(g, at):
        block = parts_ref[g, room:, :].astype(f32)
        return block[at : at + 1] + block[at + 1 : at + 2] + block[at + 2 : at + 3]

    parts = []
    for g in range(groups):
        part = parts_ref[g, :room, :]
        if g + 1 < groups:
            whole = gelu(jnp.maximum(edge(g, 0), edge(g + 1, 8))).astype(f32)
            final = count(start_row < (g + 1) * n) - count(start_row < g * n) - 1
            final = jnp.where(count(start_row == (g + 1) * n) > 0, -1, final)
            part = jnp.where(spot == final, whole, part.astype(f32)).astype(bf16)
        parts.append(part)
    out_ref[...] = dot(want_ref[...], jnp.concatenate(parts, axis=0)).astype(bf16)


def spread_kernel(rows_ref, out_ref):
    nz, per_z, width = rows_ref.shape
    parts, copies, part, _ = out_ref.shape
    n = nz * per_z
    rank = per_z // parts
    at = lax.broadcasted_iota(jnp.int32, (n, 1), 0)
    pts = at // part
    source = at % part // rank * per_z + (pts % 2 * (parts // 2) + pts // 2) * rank + at % rank
    moved = dot(one_hot(source, n), rows_ref[...].reshape(n, width)).astype(bf16)
    for i in range(parts):
        for x in range(copies):
            out_ref[i, x] = moved[i * part : (i + 1) * part]


def norm5_kernel(pick_ref, parts_ref, gain_ref, qkv_ref, q_ref, kv_ref, cols_ref):
    n = pick_ref.shape[0]
    groups, width = parts_ref.shape[1], parts_ref.shape[3]
    parts = [parts_ref[:, g].reshape(n, width) for g in range(groups)]
    own = parts_ref[:, pl.ds(lax.axis_index("x"), 1)].reshape(n, width)
    picked = dot(pick_ref[...], jnp.concatenate(parts + [own], axis=1)).astype(bf16)
    rows = picked[:, : groups * width]
    cols_ref[...] = picked[:, groups * width :]
    normed = layer_norm(rows, gain_ref[...])
    weights = jnp.concatenate([qkv_ref[i] for i in range(3)], axis=1)
    projected = dot(normed, weights).astype(bf16)
    q_ref[...] = projected[:, :width]
    kv_ref[...] = projected[:, width:]


def sum_kernel(cols_ref, parts_ref, out_ref):
    total = cols_ref[...].astype(f32)
    summed = parts_ref[0].astype(f32)
    for g in range(1, parts_ref.shape[0]):
        summed = summed + parts_ref[g].astype(f32)
    out_ref[...] = (total + summed).astype(bf16)


def shape(dims, dtype=bf16):
    return jax.ShapeDtypeStruct(dims, dtype)


def exchange(block, axes):
    return lax.all_to_all(block, axes, split_axis=0, concat_axis=0, tiled=True)


VMEM = pl.BlockSpec(memory_space=pltpu.VMEM)
HBM = pl.BlockSpec(memory_space=pltpu.HBM)
DMA = pltpu.SemaphoreType.DMA


def kernel(body, name, out_shape, scratch=(), flops=0, **extra):
    extra["cost_estimate"] = pl.CostEstimate(
        flops=flops or 1 << 28, bytes_accessed=0, transcendentals=0
    )
    return pl.pallas_call(
        body,
        out_shape=out_shape,
        scratch_shapes=list(scratch),
        compiler_params=pltpu.CompilerParams(vmem_limit_bytes=48 << 20),
        name=name,
        **extra,
    )


def local(
    feats4, order4, gain4, qkv4, proj4, pool_weight, child5, mask5, order5, gain5, qkv5, proj5
):
    n = feats4.shape[0]
    nz = lax.axis_size("z")
    planes = lax.axis_size("y") * lax.axis_size("c") * lax.axis_size("x")
    nx = lax.axis_size("x")

    feats4_pair = lax.all_gather(feats4, "c", axis=0, tiled=True)
    wanted, owner4, slot5 = kernel(
        functools.partial(request_kernel, planes),
        "request",
        [shape((nz, 4, planes // 2), jnp.int32), shape((1, n), jnp.int32), shape((1, n), jnp.int32)],
    )(jnp.stack([order4, order5]))
    by_z = exchange(wanted, ("z",)).transpose(2, 1, 0)
    by_z, feats4_pair = lax.optimization_barrier((by_z, feats4_pair))
    asked = exchange(by_z.reshape(planes // 2, 4 * nz), ("y", "x"))
    asked_both = lax.all_gather(asked, "c", axis=0, tiled=True)

    chips = n // 2
    outgoing = kernel(pick_kernel, "pick4", shape((chips, 2 * C4)))(asked, feats4_pair)
    arrived = exchange(outgoing.reshape(chips, 4, C4 // 2), CHIPS).reshape(chips, 2 * C4)
    child_rows = child5.T
    width = C5 // nx
    square = shape((n, n))
    room = n - (nx - 1) * (n // KIDS)
    room += -room % EDGE + EDGE
    pick4, pick5, want5, place, ends, gain4 = kernel(
        prepare_kernel,
        "prepare",
        [
            square,
            square,
            shape((n, nx * room)),
            shape((room, n)),
            shape((3, n, width), f32),
            shape((1, C4), f32),
        ],
    )(owner4, slot5, asked_both, child_rows, gain4.reshape(1, C4))
    curve_rows, normed4 = kernel(norm4_kernel, "norm4", [shape((n, C4)), shape((n, C4))])(
        pick4, arrived, gain4
    )
    other4 = lax.ppermute(normed4, "x", [(i, i ^ 1) for i in range(nx)])
    half = 4 * n * n * C4 * H4
    qt4, peak4, mixed4, gain5 = kernel(
        own_kernel,
        "attend4_own",
        [
            shape((C4, n)),
            shape((H4 // TOGETHER, 1, TOGETHER * n), f32),
            shape((H4 // TOGETHER, SUMS, TOGETHER * n), f32),
            shape((1, C5), f32),
        ],
        attend_scratch(H4, n, n),
        flops=half,
    )(normed4, qkv4, gain5.reshape(1, C5))
    fine_out, parts4 = kernel(
        other_kernel,
        "attend4_other",
        [shape((n, C4)), shape((nx, room + EDGE, width))],
        attend_scratch(H4, n, n)
        + [pltpu.VMEM((H4, HEAD, n), bf16), pltpu.VMEM((n, C4), bf16), DMA((1,))],
        flops=half,
        out_specs=[pl.BlockSpec(memory_space=pl.ANY), VMEM],
    )(other4, qkv4, qt4, peak4, mixed4, curve_rows, proj4, pool_weight, child_rows, place, ends)

    pooled = kernel(pool_kernel, "pool", shape((n, width)))(
        exchange(parts4, "x"), child_rows, want5
    )
    by_z = exchange(pooled.reshape(nz, n // nz, width), ("z",))
    copies = kernel(
        spread_kernel, "spread", shape((planes // nx, nx, n * nx // planes, width))
    )(by_z)
    parts5 = exchange(copies.reshape(planes, n * nx // planes, width), PLANE)
    parts5 = parts5.reshape(copies.shape)
    query5, kv5, own_columns = kernel(
        norm5_kernel,
        "norm5",
        [shape((n, width)), shape((n, 2 * width)), shape((n, width))],
    )(pick5, parts5, gain5, qkv5)
    both5 = lax.all_gather(kv5, "c", axis=0, tiled=True)
    terms = kernel(
        coarse_kernel,
        "attend5",
        shape((nx, n, width)),
        attend_scratch(width // HEAD, n, 2 * n)
        + [pltpu.VMEM((width, n), bf16), pltpu.VMEM((width // HEAD, HEAD, n), bf16)],
    )(query5, both5, proj5)
    coarse_out = kernel(sum_kernel, "add5", shape((n, width)))(own_columns, exchange(terms, "x"))
    return (fine_out, coarse_out)


def solution(mesh):
    pts, grp = mesh.devices.shape
    inner = Mesh(mesh.devices.reshape(pts // 8, 4, 2, grp), ALL)
    in_specs = (
        P(ALL, None),
        P(ALL),
        P(),
        P(),
        P(),
        P(),
        P(PTS, None),
        P(PTS, None),
        P(PTS),
        P(),
        P(None, None, "x"),
        P("x", None),
    )
    out_specs = (P(ALL, None), P(PTS, "x"))
    return jax.shard_map(local, mesh=inner, in_specs=in_specs, out_specs=out_specs, check_vma=False)
```

```python
import functools
import math

import jax
import jax.numpy as jnp
from jax import lax
from jax.experimental import pallas as pl
from jax.experimental.pallas import tpu as pltpu
from jax.sharding import Mesh
from jax.sharding import PartitionSpec as P

C4 = 256
H4 = 16
C5 = 512
H5 = 32
HEAD = 16
KIDS = 8

epsilon = 1e-05
f32 = jnp.float32
bf16 = jnp.bfloat16

PTS = ("z", "y", "c")
PLANE = ("y", "c", "x")
CHIPS = ("z", "y", "x")
ALL = ("z", "y", "c", "x")


def dot(a, b):
    return jnp.dot(a, b, preferred_element_type=f32)


def column(row):
    return jnp.transpose(jnp.broadcast_to(row, (8, row.shape[1])))[:, :1]


def one_hot(col, width):
    lanes = lax.broadcasted_iota(jnp.int32, (col.shape[0], width), 1)
    return jnp.where(col == lanes, 1.0, 0.0).astype(bf16)


def layer_norm(rows_in, norm_gain):
    values = rows_in.astype(f32)
    center = values - jnp.mean(values, axis=-1, keepdims=True)
    spread = jnp.mean(center * center, axis=-1, keepdims=True)
    return (center * lax.rsqrt(spread + epsilon) * norm_gain).astype(bf16)


def fetch(pairs, sems):
    copies = [pltpu.make_async_copy(a, b, sems.at[i]) for i, (a, b) in enumerate(pairs)]
    for copy in copies:
        copy.start()
    return copies


def request_kernel(planes, orders_ref, out_ref, owner_ref, slot_ref):
    o4, o5 = orders_ref[0:1, :], orders_ref[1:2, :]
    n = o4.shape[1]
    nz, nx = out_ref.shape[0], lax.axis_size("x")
    x = lax.axis_index("x")
    owner4, owner5 = o4 // n, o5 // n
    ny, half, per_z = planes // (2 * nx), planes // 2, planes // nx
    u = owner4 % planes
    lane4 = u // nx % 2 * half + u // (2 * nx) * nx + u % nx
    owner_ref[...] = u // nx % 2 * (n // 2) + owner4 // planes * half + lane4 % half
    of_pts = owner5 % per_z
    pair5 = of_pts % 2 * ny + of_pts // 2

    lanes = lax.broadcasted_iota(jnp.int32, (n, n), 1)
    rows = lax.broadcasted_iota(jnp.int32, (n, n), 0)
    earlier = jnp.where((column(owner5) == owner5) & (rows < lanes), 1.0, 0.0)
    rank = jnp.sum(earlier, axis=0, keepdims=True).astype(jnp.int32)
    slot_ref[...] = (of_pts * nz + owner5 // per_z) * nx + rank

    place = lax.broadcasted_iota(jnp.int32, (planes, n), 0)
    zs = lax.broadcasted_iota(jnp.int32, (nz, n), 0)

    def table(z_hit, u_hit, row):
        low = jnp.where(u_hit, (row % 256).astype(f32), 0.0)
        high = jnp.where(u_hit, (row // 256).astype(f32), 0.0)
        both = lax.dot_general(
            jnp.where(z_hit, 1.0, 0.0).astype(bf16),
            jnp.concatenate([low, high], axis=0).astype(bf16),
            (((1,), (1,)), ((), ())),
            preferred_element_type=f32,
        )
        return (both[:, :planes] + 256.0 * both[:, planes:]).astype(jnp.int32)

    want4 = table(zs == owner4 // planes, place == lane4, o4 % n)
    own_rank = (zs == owner5 // per_z) & (rank == x)
    want5 = table(own_rank, place // nx == pair5, o5 % n)
    for c in range(2):
        out_ref[:, c, :] = want4[:, c * half : (c + 1) * half]
        out_ref[:, 2 + c, :] = want5[:, c * half : (c + 1) * half]


def picks(cols, width):
    return jnp.concatenate([one_hot(cols[:, i : i + 1], width) for i in range(cols.shape[1])], axis=0)


def pick_kernel(asked_ref, table_ref, out_ref):
    nz = asked_ref.shape[1] // 4
    n, width = table_ref.shape[0] // 2, table_ref.shape[1]
    for c in range(2):
        pick = picks(asked_ref[:, c * nz : (c + 1) * nz], n)
        out_ref[:, c * width : (c + 1) * width] = dot(
            pick, table_ref[c * n : (c + 1) * n, :]
        ).astype(bf16)


def prepare_kernel(
    owner_ref,
    slot_ref,
    asked_ref,
    child_ref,
    gain_ref,
    pick4_ref,
    pick5_ref,
    want5_ref,
    place_ref,
    ends_ref,
    gain_out_ref,
):
    gain_out_ref[...] = gain_ref[...]
    n = owner_ref.shape[1]
    points = child_ref.shape[1]
    pick4_ref[...] = one_hot(column(owner_ref[...]), n)
    pick5_ref[...] = one_hot(column(slot_ref[...]), n)

    start_row = run_starts(child_ref, n)
    room = place_ref.shape[0]
    at = lax.broadcasted_iota(jnp.int32, (1, points), 1)
    for g in range(want5_ref.shape[1] // room):
        before = count(start_row < g * n)
        at = jnp.where(start_row // n == g, at - before + g * room, at)
    nz = asked_ref.shape[1] // 4
    asked5 = jnp.where(
        lax.axis_index("c") == 0, asked_ref[:, 2 * nz : 3 * nz], asked_ref[:, 3 * nz :]
    )
    wanted = picks(asked5, points).astype(f32)
    spot = jnp.sum(wanted * at.astype(f32), axis=1, keepdims=True).astype(jnp.int32)
    want5_ref[...] = one_hot(spot, want5_ref.shape[1])

    own_row = own_starts(child_ref, n)
    own = column(own_row)
    lanes = lax.broadcasted_iota(jnp.int32, (points, n), 1)
    opened = jnp.where((own >= 0) & (own <= lanes), 1.0, 0.0)
    number = jnp.sum(opened, axis=0, keepdims=True).astype(jnp.int32) - 1
    opens_here = jnp.sum(jnp.where(own == lanes, 1.0, 0.0), axis=0, keepdims=True)
    spots = lax.broadcasted_iota(jnp.int32, (room, n), 0)
    place_ref[...] = jnp.where((spots == number) & (opens_here > 0.0), 1.0, 0.0).astype(bf16)

    rows = lax.broadcasted_iota(jnp.int32, (n, points), 0)
    first = jnp.where(own_row == rows, 1.0, 0.0).astype(bf16)
    opens = dot(first, jnp.ones((points, ends_ref.shape[2]), bf16))
    cut = ahead(opens, 1, 1.0)
    for i in range(ends_ref.shape[0]):
        ends_ref[i] = cut
        cut = jnp.maximum(cut, ahead(cut, 1 << i, 1.0))


def norm4_kernel(pick_ref, arrived_ref, gain_ref, rows_ref, normed_ref):
    width = rows_ref.shape[1]
    arrived = jnp.concatenate([arrived_ref[:, :width], arrived_ref[:, width:]], axis=0)
    rows = dot(pick_ref[...], arrived).astype(bf16)
    rows_ref[...] = rows
    normed_ref[...] = layer_norm(rows, gain_ref[...])


TOGETHER = 2
SUMS = (TOGETHER + 1) * HEAD


def attend(heads, k_ref, qt_ref, vt_ref, s_ref, finish, before=None, chunk=512):
    queries = s_ref.shape[2]
    together = queries // qt_ref.shape[1]
    steps = heads // together
    keys = k_ref.shape[0]
    row_head = lax.broadcasted_iota(jnp.int32, qt_ref.shape, 0) // HEAD

    def of_step(step):
        q = qt_ref[...]
        none = jnp.zeros_like(q)
        each = [jnp.where(row_head == step * together + i, q, none) for i in range(together)]
        return jnp.concatenate(each, axis=1)

    def score(q_head, slot, c, top):
        s = dot(k_ref[c * chunk : (c + 1) * chunk, :], q_head)
        s_ref[slot, c * chunk : (c + 1) * chunk, :] = s
        return jnp.maximum(top, jnp.max(s.reshape(chunk // 8, 8, queries), axis=0))

    def low():
        return jnp.full((8, queries), -jnp.inf, f32)

    def step(head, slot, peak, more):
        if before is None:
            mixed = jnp.zeros((vt_ref.shape[1], queries), f32)
        else:
            earlier, mixed = before(head)
            peak = jnp.maximum(peak, earlier)
            mixed = mixed * jnp.exp(earlier - peak)
        top = low()
        q_next = of_step(head + 1) if more else None
        for c in range(keys // chunk):
            if more:
                top = score(q_next, 1 - slot, c, top)
            p = jnp.exp(s_ref[slot, c * chunk : (c + 1) * chunk, :] - peak).astype(bf16)
            mixed = mixed + dot(vt_ref[head, :, c * chunk : (c + 1) * chunk], p)
        finish(head, peak, mixed)
        return jnp.max(top, axis=0, keepdims=True)

    top = low()
    q_first = of_step(0)
    for c in range(keys // chunk):
        top = score(q_first, 0, c, top)
    peak = jnp.max(top, axis=0, keepdims=True)

    def pair(i, peak):
        peak = step(2 * i, 0, peak, True)
        return step(2 * i + 1, 1, peak, True)

    peak = lax.fori_loop(0, steps // 2 - 1, pair, peak)
    peak = step(steps - 2, 0, peak, True)
    step(steps - 1, 1, peak, False)


def divide(at_ref):
    n = at_ref.shape[2]

    def finish(step, peak, mixed):
        together = mixed.shape[1] // n
        for i in range(together):
            part = mixed[i * HEAD : (i + 1) * HEAD, i * n : (i + 1) * n]
            total = mixed[together * HEAD :, i * n : (i + 1) * n]
            at_ref[step * together + i] = (part / total).astype(bf16)

    return finish


def joined(at_ref):
    heads, size, queries = at_ref.shape
    return jnp.transpose(at_ref[...].reshape(heads * size, queries))


def attend_scratch(heads, queries, keys, together):
    width = heads * HEAD
    return [
        pltpu.VMEM((keys, width), bf16),
        pltpu.VMEM((heads // together, (together + 1) * HEAD, keys), bf16),
        pltpu.VMEM((2, keys, together * queries), f32),
    ]


def load_values(vt_ref, values, heads):
    keys = values.shape[1]
    own = vt_ref.shape[1] - HEAD
    vt_ref[:, :own, :] = values.reshape(vt_ref.shape[0], own, keys)
    vt_ref[:, own:, :] = jnp.ones((vt_ref.shape[0], HEAD, keys), bf16)


SCALE = 1.0 / math.sqrt(HEAD)


def across(weights, rows):
    return lax.dot_general(weights, rows, (((0,), (1,)), ((), ())), preferred_element_type=f32)


def own_kernel(
    own_ref, qkv_ref, gain_ref, qt_ref, peak_ref, mixed_ref, gain_out_ref, k, vt, s
):
    own = own_ref[...]
    gain_out_ref[...] = gain_ref[...]
    qt_ref[...] = across(qkv_ref[0], own).astype(bf16) * bf16(SCALE)
    k[...] = dot(own, qkv_ref[1]).astype(bf16)
    load_values(vt, across(qkv_ref[2], own).astype(bf16), H4)

    def finish(head, peak, mixed):
        peak_ref[head] = peak
        mixed_ref[head] = mixed

    attend(H4, k, qt_ref, vt, s, finish)


def other_kernel(
    other_ref,
    qkv_ref,
    qt_ref,
    peak_ref,
    mixed_ref,
    rows_ref,
    proj_ref,
    weight_ref,
    child_ref,
    place_ref,
    ends_ref,
    out_ref,
    parts_ref,
    k,
    vt,
    s,
    at,
    fine_ref,
    sems,
):
    other = other_ref[...]
    k[...] = dot(other, qkv_ref[1]).astype(bf16)
    load_values(vt, across(qkv_ref[2], other).astype(bf16), H4)
    attend(H4, k, qt_ref, vt, s, divide(at), lambda head: (peak_ref[head], mixed_ref[head]))
    fine = (rows_ref[...].astype(f32) + dot(joined(at), proj_ref[...])).astype(bf16)
    fine_ref[...] = fine
    copies = fetch([(fine_ref, out_ref)], sems)
    pool_own(fine, weight_ref, child_ref, place_ref, ends_ref, parts_ref)
    copies[0].wait()


def coarse_kernel(q_ref, both_ref, proj_ref, out_ref, k, vt, s, qt, at):
    n, width = q_ref.shape
    qt[...] = jnp.transpose(q_ref[...] * bf16(SCALE))
    k[...] = both_ref[:, :width]
    values = both_ref[:, width:]
    load_values(vt, jnp.transpose(values), width // HEAD)
    attend(width // HEAD, k, qt, vt, s, divide(at))
    terms = dot(joined(at), proj_ref[...]).astype(bf16)
    parts = out_ref.shape[0]
    for g in range(parts):
        out_ref[g] = terms[:, g * width : (g + 1) * width]


EDGE = 16


def gelu(values):
    return jax.nn.gelu(values, approximate=True).astype(bf16)


def three_terms(value):
    first = value.astype(bf16).astype(f32)
    second = (value - first).astype(bf16).astype(f32)
    return [first, second, value - first - second]


def run_starts(child_ref, n):
    nx = lax.axis_size("x")
    return child_ref[0:1, :] - lax.axis_index(PTS) * (nx * n)


def own_starts(child_ref, n):
    return run_starts(child_ref, n) - lax.axis_index("x") * n


def ahead(block, k, fill):
    return jnp.concatenate([block[k:], jnp.full((k, block.shape[1]), fill, f32)], axis=0)


def pool_own(fine, weight_ref, child_ref, place_ref, ends_ref, parts_ref):
    n = fine.shape[0]
    groups, total, width = parts_ref.shape
    room = total - EDGE
    start_row = own_starts(child_ref, n)
    last = jnp.max(
        jnp.where(start_row < n, start_row.astype(f32), -1.0), axis=1, keepdims=True
    ).astype(jnp.int32)
    tail = KIDS
    leaving = lax.broadcasted_iota(jnp.int32, (tail, width), 0) + (n - tail) >= last
    edge_row = lax.broadcasted_iota(jnp.int32, (EDGE, width), 0)
    ends = [ends_ref[i] > 0.0 for i in range(ends_ref.shape[0])]
    for g in range(groups):
        best = dot(fine, weight_ref[:, g * width : (g + 1) * width])
        lifted_tail = best[n - tail :]
        for i, end in enumerate(ends):
            best = jnp.where(end, best, jnp.maximum(best, ahead(best, 1 << i, 0.0)))
        parts_ref[g, :room, :] = dot(place_ref[...], gelu(best)).astype(bf16)
        head = jnp.max(jnp.where(leaving, lifted_tail, -jnp.inf), axis=0, keepdims=True)
        edge = jnp.zeros((EDGE, width), f32)
        for at, value in ((0, head), (8, best[0:1])):
            for i, term in enumerate(three_terms(value)):
                edge = jnp.where(edge_row == at + i, term, edge)
        parts_ref[g, room:, :] = edge.astype(bf16)


def count(hits):
    return jnp.sum(jnp.where(hits, 1.0, 0.0), axis=1, keepdims=True).astype(jnp.int32)


def pool_kernel(parts_ref, child_ref, want_ref, out_ref):
    groups, total, width = parts_ref.shape
    room = total - EDGE
    n = out_ref.shape[0]
    start_row = run_starts(child_ref, n)
    spot = lax.broadcasted_iota(jnp.int32, (room, width), 0)

    def edge(g, at):
        block = parts_ref[g, room:, :].astype(f32)
        return block[at : at + 1] + block[at + 1 : at + 2] + block[at + 2 : at + 3]

    parts = []
    for g in range(groups):
        part = parts_ref[g, :room, :]
        if g + 1 < groups:
            whole = gelu(jnp.maximum(edge(g, 0), edge(g + 1, 8))).astype(f32)
            final = count(start_row < (g + 1) * n) - count(start_row < g * n) - 1
            final = jnp.where(count(start_row == (g + 1) * n) > 0, -1, final)
            part = jnp.where(spot == final, whole, part.astype(f32)).astype(bf16)
        parts.append(part)
    out_ref[...] = dot(want_ref[...], jnp.concatenate(parts, axis=0)).astype(bf16)


def spread_kernel(rows_ref, out_ref):
    nz, per_z, width = rows_ref.shape
    parts, copies, part, _ = out_ref.shape
    n = nz * per_z
    rank = per_z // parts
    at = lax.broadcasted_iota(jnp.int32, (n, 1), 0)
    pts = at // part
    source = at % part // rank * per_z + (pts % 2 * (parts // 2) + pts // 2) * rank + at % rank
    moved = dot(one_hot(source, n), rows_ref[...].reshape(n, width)).astype(bf16)
    for i in range(parts):
        for x in range(copies):
            out_ref[i, x] = moved[i * part : (i + 1) * part]


def norm5_kernel(pick_ref, parts_ref, gain_ref, qkv_ref, q_ref, kv_ref, cols_ref):
    n = pick_ref.shape[0]
    groups, width = parts_ref.shape[1], parts_ref.shape[3]
    parts = [parts_ref[:, g].reshape(n, width) for g in range(groups)]
    own = parts_ref[:, pl.ds(lax.axis_index("x"), 1)].reshape(n, width)
    picked = dot(pick_ref[...], jnp.concatenate(parts + [own], axis=1)).astype(bf16)
    rows = picked[:, : groups * width]
    cols_ref[...] = picked[:, groups * width :]
    normed = layer_norm(rows, gain_ref[...])
    weights = jnp.concatenate([qkv_ref[i] for i in range(3)], axis=1)
    projected = dot(normed, weights).astype(bf16)
    q_ref[...] = projected[:, :width]
    kv_ref[...] = projected[:, width:]


def sum_kernel(cols_ref, parts_ref, out_ref):
    total = cols_ref[...].astype(f32)
    summed = parts_ref[0].astype(f32)
    for g in range(1, parts_ref.shape[0]):
        summed = summed + parts_ref[g].astype(f32)
    out_ref[...] = (total + summed).astype(bf16)


def shape(dims, dtype=bf16):
    return jax.ShapeDtypeStruct(dims, dtype)


def exchange(block, axes):
    return lax.all_to_all(block, axes, split_axis=0, concat_axis=0, tiled=True)


VMEM = pl.BlockSpec(memory_space=pltpu.VMEM)
HBM = pl.BlockSpec(memory_space=pltpu.HBM)
DMA = pltpu.SemaphoreType.DMA


def kernel(body, name, out_shape, scratch=(), flops=0, **extra):
    extra["cost_estimate"] = pl.CostEstimate(
        flops=flops or 1 << 28, bytes_accessed=0, transcendentals=0
    )
    return pl.pallas_call(
        body,
        out_shape=out_shape,
        scratch_shapes=list(scratch),
        compiler_params=pltpu.CompilerParams(vmem_limit_bytes=48 << 20),
        name=name,
        **extra,
    )


def local(
    feats4, order4, gain4, qkv4, proj4, pool_weight, child5, mask5, order5, gain5, qkv5, proj5
):
    n = feats4.shape[0]
    nz = lax.axis_size("z")
    planes = lax.axis_size("y") * lax.axis_size("c") * lax.axis_size("x")
    nx = lax.axis_size("x")

    feats4_pair = lax.all_gather(feats4, "c", axis=0, tiled=True)
    wanted, owner4, slot5 = kernel(
        functools.partial(request_kernel, planes),
        "request",
        [shape((nz, 4, planes // 2), jnp.int32), shape((1, n), jnp.int32), shape((1, n), jnp.int32)],
    )(jnp.stack([order4, order5]))
    by_z = exchange(wanted, ("z",)).transpose(2, 1, 0)
    by_z, feats4_pair = lax.optimization_barrier((by_z, feats4_pair))
    asked = exchange(by_z.reshape(planes // 2, 4 * nz), ("y", "x"))
    asked_both = lax.all_gather(asked, "c", axis=0, tiled=True)

    chips = n // 2
    outgoing = kernel(pick_kernel, "pick4", shape((chips, 2 * C4)))(asked, feats4_pair)
    arrived = exchange(outgoing.reshape(chips, 4, C4 // 2), CHIPS).reshape(chips, 2 * C4)
    child_rows = child5.T
    width = C5 // nx
    square = shape((n, n))
    room = n - (nx - 1) * (n // KIDS)
    room += -room % EDGE + EDGE
    pick4, pick5, want5, place, ends, gain4 = kernel(
        prepare_kernel,
        "prepare",
        [
            square,
            square,
            shape((n, nx * room)),
            shape((room, n)),
            shape((3, n, width), f32),
            shape((1, C4), f32),
        ],
    )(owner4, slot5, asked_both, child_rows, gain4.reshape(1, C4))
    curve_rows, normed4 = kernel(norm4_kernel, "norm4", [shape((n, C4)), shape((n, C4))])(
        pick4, arrived, gain4
    )
    other4 = lax.ppermute(normed4, "x", [(i, i ^ 1) for i in range(nx)])
    half = 4 * n * n * C4 * H4
    qt4, peak4, mixed4, gain5 = kernel(
        own_kernel,
        "attend4_own",
        [
            shape((C4, n)),
            shape((H4 // TOGETHER, 1, TOGETHER * n), f32),
            shape((H4 // TOGETHER, SUMS, TOGETHER * n), f32),
            shape((1, C5), f32),
        ],
        attend_scratch(H4, n, n, TOGETHER),
        flops=half,
    )(normed4, qkv4, gain5.reshape(1, C5))
    fine_out, parts4 = kernel(
        other_kernel,
        "attend4_other",
        [shape((n, C4)), shape((nx, room + EDGE, width))],
        attend_scratch(H4, n, n, TOGETHER)
        + [pltpu.VMEM((H4, HEAD, n), bf16), pltpu.VMEM((n, C4), bf16), DMA((1,))],
        flops=half,
        out_specs=[pl.BlockSpec(memory_space=pl.ANY), VMEM],
    )(other4, qkv4, qt4, peak4, mixed4, curve_rows, proj4, pool_weight, child_rows, place, ends)

    pooled = kernel(pool_kernel, "pool", shape((n, width)))(
        exchange(parts4, "x"), child_rows, want5
    )
    by_z = exchange(pooled.reshape(nz, n // nz, width), ("z",))
    copies = kernel(
        spread_kernel, "spread", shape((planes // nx, nx, n * nx // planes, width))
    )(by_z)
    parts5 = exchange(copies.reshape(planes, n * nx // planes, width), PLANE)
    parts5 = parts5.reshape(copies.shape)
    query5, kv5, own_columns = kernel(
        norm5_kernel,
        "norm5",
        [shape((n, width)), shape((n, 2 * width)), shape((n, width))],
    )(pick5, parts5, gain5, qkv5)
    both5 = lax.all_gather(kv5, "c", axis=0, tiled=True)
    terms = kernel(
        coarse_kernel,
        "attend5",
        shape((nx, n, width)),
        attend_scratch(width // HEAD, n, 2 * n, 1)
        + [pltpu.VMEM((width, n), bf16), pltpu.VMEM((width // HEAD, HEAD, n), bf16)],
    )(query5, both5, proj5)
    coarse_out = kernel(sum_kernel, "add5", shape((n, width)))(own_columns, exchange(terms, "x"))
    return (fine_out, coarse_out)


def solution(mesh):
    pts, grp = mesh.devices.shape
    inner = Mesh(mesh.devices.reshape(pts // 8, 4, 2, grp), ALL)
    in_specs = (
        P(ALL, None),
        P(ALL),
        P(),
        P(),
        P(),
        P(),
        P(PTS, None),
        P(PTS, None),
        P(PTS),
        P(),
        P(None, None, "x"),
        P("x", None),
    )
    out_specs = (P(ALL, None), P(PTS, "x"))
    return jax.shard_map(local, mesh=inner, in_specs=in_specs, out_specs=out_specs, check_vma=False)
```
